32 devices in a mesh: groups: 2 (over y), ctx: 4 (over z), head: 2 (over x), user: 2 (over core).
Axes of the slice: x: 2, y: 2, z: 4, core: 2. Of those that a mesh axis runs over, the one named last changes fastest.
Arguments:
- projected: bfloat16 [4, 2048, 8, 4, 128], P(('groups', 'user'), 'ctx', 'head'), parts along dimension 0, may hold values from -6 to 6
- upstream: bfloat16 [4, 2048, 8, 128], P(('groups', 'user'), 'ctx', 'head'), parts along dimension 0, may hold values from -6 to 6
- ips_weight: float32 [4, 2048], P(('groups', 'user')), parts along dimension 0, may hold values from 0.2 to 5
- item_ids: int32 [4, 2048], P(('groups', 'user')), parts along dimension 0, may hold values from 0 to 999
- session_ids: int32 [4, 2048], P(('groups', 'user')), parts along dimension 0, may hold values from 0 to 7, never falling along the last dimension, each value on 1 to 1024 neighbouring positions
- session_blocks: int32 [4, 4, 3], P(('groups', 'user')), parts along dimension 0, may hold values from -1 to 1, as said below
Outputs:
- mixed: bfloat16 [4, 2048, 8, 128], P(('groups', 'user'), 'ctx', 'head'), parts along dimension 0
- proj_grad: bfloat16 [4, 2048, 8, 4, 128], P(('groups', 'user'), 'ctx', 'head'), parts along dimension 0
The draws below stay inside these ranges and needn't reach their ends.
There are 2 independent parts, one for each index of `groups`. The reference program is written for one: setup_inputs(seed, part) draws one part's arguments, and reference() takes and returns one part's arrays. A program takes and returns all parts, laid end to end along the dimension named above; each array names one. Nothing has to cross between parts.
Inputs may be any that keep to these rules, and one draw needn't show every extreme that they name: `session_blocks`: row b lists, in ascending order, distinct blocks below b, and -1 in the remaining slots; row 3 always lists block 1 and never block 2, and row 1 never lists block 0.
All inputs are finite; a program needn't handle non-finite values.
Results may differ from the reference program's by a relative error of at most 0.0056.
Values may be sent and summed in bfloat16 or wider, within the bound.
A program may use at most 128 MiB of HBM per device.

```python
import math
import jax
import jax.numpy as jnp
import numpy as np
from jax import lax

H = 8
DH = 128
BLOCK = 512
USERS = 2
NB = 4
L = 2048
SLOTS = 3


def draw_session_blocks(key, part):
    key_rate, key_roll = jax.random.split(jax.random.fold_in(key, 17))
    rates = jax.random.randint(key_rate, (USERS, NB, 1), 30, 71)
    rolls = jax.random.randint(key_roll, (USERS, NB, NB), 0, 100)
    rows_b = jnp.arange(NB, dtype=jnp.int32)[:, None]
    cols_c = jnp.arange(NB, dtype=jnp.int32)[None, :]
    allowed = cols_c <= rows_b - 1
    forced = (rows_b == NB - 1) & (cols_c == NB - 3)
    barred = (rows_b == 1) & (cols_c == 0) | (rows_b == NB - 1) & (cols_c == NB - 2)
    chosen = allowed & ((rolls < rates) | forced) & jnp.logical_not(barred)
    order = jnp.where(chosen, cols_c, NB + cols_c)
    ranked = jnp.sort(order, axis=-1)[..., :SLOTS]
    return jnp.where(ranked < NB, ranked, -1).astype(jnp.int32)


def touch_ends(entries, rng, low, high):
    dims = entries.shape
    spot = [jax.random.randint(jax.random.fold_in(rng, axis), (), 0, dims[axis]) for axis in range(len(dims))]
    entries = entries.at[tuple(spot)].set(low)
    longest = dims.index(max(dims))
    spot[longest] = (spot[longest] + 1) % dims[longest]
    return entries.at[tuple(spot)].set(high)


def shard_levels(stream_key, dims, cuts, low, top_value):
    loudness, own = 1.0, jax.random.fold_in(stream_key, 6)
    for position, blocks in cuts:
        heights = jnp.exp(jax.random.uniform(jax.random.fold_in(own, position), (blocks,), jnp.float32, low / len(cuts), top_value / len(cuts)))
        loudness = loudness * jnp.repeat(heights, dims[position] // blocks).reshape([-1 if axis == position else 1 for axis in range(len(dims))])
    return loudness


def cumulative_ranks(amount, skew):
    weights = [(1 << 20) // math.isqrt(standing ** skew) + 1 for standing in range(1, amount + 1)]
    spread = 1 + sum(weights) // (1 << 30)
    return np.cumsum(np.array([max(1, weight // spread) for weight in weights]))


def ranked_ids(key, dims, count, skew):
    grid = cumulative_ranks(count, skew)
    ticket = jax.random.randint(jax.random.fold_in(key, 1), dims, 0, int(grid[count - 1]))
    rank = jnp.searchsorted(jnp.asarray(grid, jnp.int32), ticket, side="right")
    return jax.random.permutation(jax.random.fold_in(key, 2), count)[rank].astype(jnp.int32)


def profile(count, total, bound, lean):
    loads = [(1 << 20) // math.isqrt(grade ** lean) + 1 for grade in range(2, count + 1)]
    spare, counts = total - bound - (count - 1), [1] * (count - 1)
    while spare > 0:
        free = [i for i in range(count - 1) if counts[i] < bound]
        mass, remaining = sum([loads[i] for i in free]), spare
        for i in free:
            more = min(bound - counts[i], max(1, remaining * loads[i] // mass), spare)
            counts[i] = counts[i] + more
            spare = spare - more
    return np.array([bound] + counts)


def ragged_sizes(rng, amount, total, reach, skew):
    if amount == 2:
        one = jax.random.randint(rng, (), max(1, total - reach), min(reach, total - 1) + 1)
        return jnp.stack([one, total - one])
    sizes = jnp.asarray(profile(amount, total, reach, skew), jnp.int32)
    twos = (amount - 1) // 2
    donor, sink = sizes[1:1 + 2 * twos:2], sizes[2:2 + 2 * twos:2]
    margin = jnp.minimum(donor - 1, reach - sink)
    moved = jax.random.randint(jax.random.fold_in(rng, 1), (twos,), 0, 1 << 20) % (margin + 1)
    sizes = sizes.at[1:1 + 2 * twos:2].set(donor - moved).at[2:2 + 2 * twos:2].set(sink + moved)
    return sizes[jax.random.permutation(jax.random.fold_in(rng, 2), amount)]


def normal_values(own_key, shape, deviation, reach, cuts=(), held_as=jnp.bfloat16):
    values = deviation * jax.random.normal(own_key, shape, jnp.float32)
    if cuts:
        values = values * shard_levels(own_key, shape, cuts, -0.22, 0.18)
    return jnp.clip(values, -reach, reach).astype(held_as)


def setup_inputs(seed: int = 0, part: int = 0) -> dict:
    splits = jax.random.split(jax.random.key(seed), 7)
    part_keys = jax.random.split(jax.random.fold_in(splits[6], part), 7)
    projected = normal_values(part_keys[0], (USERS, L, H, 4, DH), 1.0, 6.0, ((0, 2), (1, 4), (2, 2)))
    upstream = normal_values(part_keys[1], (USERS, L, H, DH), 1.0, 6.0, ((0, 2), (1, 4), (2, 2)))
    ips_weight = jnp.clip(jnp.exp(math.log(5.0) - 3.218876 * jax.random.uniform(part_keys[2], (USERS, L), jnp.float32) ** shard_levels(part_keys[2], (USERS, L), ((0, 2),), -0.2, 0.2)), 0.2, 5.0)
    item_ids = touch_ends(ranked_ids(part_keys[3], (USERS, L), 1000, 3), jax.random.fold_in(part_keys[3], 3), 0, 999).astype(jnp.int32)
    session_ids = jax.vmap(lambda own: jnp.searchsorted(jnp.cumsum(ragged_sizes(own, 2 * NB, L, 2 * BLOCK, 2)), jnp.arange(L), side="right"))(jax.random.split(part_keys[4], USERS)).reshape((USERS, L)).astype(jnp.int32)
    session_blocks = draw_session_blocks(jax.random.fold_in(jax.random.fold_in(splits[6], part), 71), part)
    return {"projected": projected, "upstream": upstream, "ips_weight": ips_weight, "item_ids": item_ids, "session_ids": session_ids, "session_blocks": session_blocks}


def block_scores(queries, keys):
    return jnp.einsum('ahd,chd->hac', queries.astype(jnp.float32), keys.astype(jnp.float32)) * DH ** (-0.5)

def visible_mask(block_q, block_k, sessions, list_row):
    inner = jnp.arange(BLOCK).astype(jnp.int32)
    pos_q = block_q * BLOCK + inner
    pos_k = block_k * BLOCK + inner
    sess_q = lax.dynamic_slice_in_dim(sessions, (block_q * BLOCK).astype(jnp.int32), BLOCK)
    sess_k = lax.dynamic_slice_in_dim(sessions, (block_k * BLOCK).astype(jnp.int32), BLOCK)
    window = (pos_k[None, :] <= pos_q[:, None]) & (pos_q[:, None] - pos_k[None, :] < BLOCK)
    window = window & (sess_q[:, None] == sess_k[None, :])
    listed = jnp.any(list_row == block_k)
    return (window | listed, (block_k == block_q) | (block_k == block_q - 1) | listed)

def one_user(rows, upstream, weights, items, sessions, lists):
    gates = rows[:, :, 0]
    q_blocks = rows[:, :, 1].reshape(NB, BLOCK, H, DH)
    k_blocks = rows[:, :, 2].reshape(NB, BLOCK, H, DH)
    v_blocks = rows[:, :, 3].reshape(NB, BLOCK, H, DH)

    def forward_block(block_q):

        def over(block_k, acc):
            block_k = jnp.asarray(block_k).astype(jnp.int32)
            vis, active = visible_mask(block_q, block_k, sessions, lists[block_q])

            def add(value):
                scores = block_scores(q_blocks[block_q], k_blocks[block_k])
                probs = jnp.where(vis[None], jax.nn.silu(scores), 0.0).astype(jnp.bfloat16)
                return value + jnp.einsum('hac,chd->ahd', probs.astype(jnp.float32), v_blocks[block_k].astype(jnp.float32))
            return lax.cond(active, add, lambda value: value, acc)
        return lax.fori_loop(0, NB, over, jnp.zeros((BLOCK, H, DH), jnp.float32))
    attended = lax.map(forward_block, jnp.arange(NB).astype(jnp.int32)).reshape(L, H, DH)
    centre = lax.optimization_barrier(jnp.mean(attended, -1, keepdims=True))
    shifted = attended - centre
    inv_std = lax.rsqrt(lax.optimization_barrier(jnp.mean(shifted * shifted, -1, keepdims=True)) + 1e-05)
    normed = shifted * inv_std
    gates_f = gates.astype(jnp.float32)
    mixed = (normed * gates_f).astype(jnp.bfloat16)
    fresh = jnp.concatenate([(items[1:] != items[:-1]).astype(jnp.float32), jnp.zeros((1,), jnp.float32)])
    scaled = weights * fresh * L / jnp.sum(weights)
    grad_mixed = scaled[:, None, None] * upstream.astype(jnp.float32)
    grad_gates = (grad_mixed * normed).astype(jnp.bfloat16)
    grad_normed = grad_mixed * gates_f
    grad_att = inv_std * (grad_normed - lax.optimization_barrier(jnp.mean(grad_normed, -1, keepdims=True)) - normed * lax.optimization_barrier(jnp.mean(grad_normed * normed, -1, keepdims=True)))
    g_blocks = grad_att.astype(jnp.bfloat16).reshape(NB, BLOCK, H, DH)

    def backward_block(key_grads, block_q):

        def over(block_k, state):
            block_k = jnp.asarray(block_k).astype(jnp.int32)
            vis, active = visible_mask(block_q, block_k, sessions, lists[block_q])

            def add(inner_state):
                grad_q, grads_kv = inner_state
                queries = q_blocks[block_q].astype(jnp.float32)
                grad_rows = g_blocks[block_q].astype(jnp.float32)
                keys = k_blocks[block_k].astype(jnp.float32)
                values = v_blocks[block_k].astype(jnp.float32)
                scores = block_scores(q_blocks[block_q], k_blocks[block_k])
                sigma = jax.nn.sigmoid(scores)
                probs = jnp.where(vis[None], jax.nn.silu(scores), 0.0).astype(jnp.bfloat16).astype(jnp.float32)
                slope = sigma * (1.0 + scores * (1.0 - sigma))
                dprod = jnp.einsum('ahd,chd->hac', grad_rows, values)
                edges = jnp.where(vis[None], dprod * slope, 0.0).astype(jnp.bfloat16).astype(jnp.float32)
                new_q = grad_q + jnp.einsum('hac,chd->ahd', edges, keys) * DH ** (-0.5)
                grad_k = jnp.einsum('hac,ahd->chd', edges, queries) * DH ** (-0.5)
                grad_v = jnp.einsum('hac,ahd->chd', probs, grad_rows)
                slot = lax.dynamic_index_in_dim(grads_kv, block_k, 0, keepdims=False) + jnp.stack([grad_k, grad_v], 2)
                return (new_q, lax.dynamic_update_index_in_dim(grads_kv, slot, block_k, 0))
            return lax.cond(active, add, lambda inner_state: inner_state, state)
        grad_q, key_grads = lax.fori_loop(0, NB, over, (jnp.zeros((BLOCK, H, DH), jnp.float32), key_grads))
        return (key_grads, grad_q)
    key_grads, grad_q = lax.scan(backward_block, jnp.zeros((NB, BLOCK, H, 2, DH), jnp.float32), jnp.arange(NB).astype(jnp.int32))
    grad_q = grad_q.reshape(L, H, DH).astype(jnp.bfloat16)
    key_grads = key_grads.reshape(L, H, 2, DH).astype(jnp.bfloat16)
    result = jnp.concatenate([grad_gates[:, :, None], grad_q[:, :, None], key_grads], 2)
    return (mixed, result)

def reference(projected, upstream, ips_weight, item_ids, session_ids, session_blocks):
    mixed_all = []
    grads_all = []
    for user in range(USERS):
        mixed, result = one_user(projected[user], upstream[user], ips_weight[user], item_ids[user], session_ids[user], session_blocks[user])
        mixed_all.append(mixed)
        grads_all.append(result)
    return (jnp.stack(mixed_all, 0), jnp.stack(grads_all, 0))
```

```python
import functools
import jax
import jax.numpy as jnp
from jax import lax
from jax.experimental import pallas as pl
from jax.experimental.pallas import tpu as pltpu
from jax.sharding import PartitionSpec as P

BLOCK = 512


def shifted_2(block, axis, distance):
    devices = range(lax.axis_size(axis))
    route = [(i - distance, i) for i in devices if i - distance in devices]
    return lax.ppermute(block, axis, route)


def pair_scores(queries, keys):
    scale = queries.shape[-1] ** (-0.5)
    return jnp.einsum("ahd,chd->hac", queries, keys, preferred_element_type=jnp.float32) * scale


def attend(queries, keys, values, visible):
    scores = pair_scores(queries, keys)
    probs = jnp.where(visible[None], jax.nn.silu(scores), 0.0).astype(jnp.bfloat16)
    return jnp.einsum("hac,chd->ahd", probs, values, preferred_element_type=jnp.float32)


def attend_back(queries, grad_rows, keys, values, visible):
    scale = queries.shape[-1] ** (-0.5)
    scores = pair_scores(queries, keys)
    sigma = jax.nn.sigmoid(scores)
    probs = jnp.where(visible[None], jax.nn.silu(scores), 0.0).astype(jnp.bfloat16)
    slope = sigma * (1.0 + scores * (1.0 - sigma))
    dprod = jnp.einsum("ahd,chd->hac", grad_rows, values, preferred_element_type=jnp.float32)
    edges = jnp.where(visible[None], dprod * slope, 0.0).astype(jnp.bfloat16)
    grad_q = jnp.einsum("hac,chd->ahd", edges, keys, preferred_element_type=jnp.float32) * scale
    grad_k = jnp.einsum("hac,ahd->chd", edges, queries, preferred_element_type=jnp.float32) * scale
    grad_v = jnp.einsum("hac,ahd->chd", probs, grad_rows, preferred_element_type=jnp.float32)
    return (grad_q, grad_k, grad_v)


def shards(projected, upstream, ips_weight, item_ids, session_ids, session_blocks):
    rows = projected[0]
    count = rows.shape[0]
    heads = rows.shape[1]
    width = rows.shape[3]
    block = BLOCK
    local_blocks = count // block
    ctx_rank = lax.axis_index("ctx")
    first = ctx_rank * local_blocks
    sessions = session_ids[0]
    lists = session_blocks[0]
    gates = rows[:, :, 0]
    queries = rows[:, :, 1].reshape(local_blocks, block, heads, width)
    pairs = rows[:, :, 2:4]
    pair_blocks = pairs.reshape(local_blocks, block, heads, 2, width)
    inner = jnp.arange(block)
    below = inner[None, :] <= inner[:, None]
    everything = jnp.ones((block, block), bool)

    def session_slice(index):
        return lax.dynamic_slice_in_dim(sessions, jnp.maximum(index, 0) * block, block)

    list_rows = []
    local = 0
    glob = first + local
    here = session_slice(glob)
    there = session_slice(glob - 1)
    list_row = lax.dynamic_index_in_dim(lists, glob, 0, keepdims=False)
    prev_listed = jnp.any(list_row == glob - 1)
    own_masks = [below & (here[:, None] == here[None, :])]
    prev_masks = [
        jnp.logical_not(below)
        & (here[:, None] == there[None, :])
        & (glob > 0)
        & jnp.logical_not(prev_listed)
    ]
    list_rows.append(list_row)
    previous = shifted_2(pair_blocks[local_blocks - 1], "ctx", 1)
    prior = [previous] + [pair_blocks[local] for local in range(local_blocks - 1)]
    local = 0
    current = pair_blocks[local]
    total = attend(queries[local], current[:, :, 0], current[:, :, 1], own_masks[local])
    total = total + attend(
        queries[local], prior[local][:, :, 0], prior[local][:, :, 1], prev_masks[local]
    )
    totals = [total]
    piece_blocks = lax.all_gather(pairs, "ctx", axis=0, tiled=True).reshape(
        -1, block, heads, 2, width
    )

    def visit(index, acc):
        chosen = lax.dynamic_index_in_dim(piece_blocks, index, 0, keepdims=False)
        local = 0
        hit = jnp.any(list_rows[local] == index)
        updated = [
            lax.cond(
                hit,
                lambda value, local=local: value
                + attend(queries[local], chosen[:, :, 0], chosen[:, :, 1], everything),
                lambda value: value,
                acc[local],
            )
        ]
        return tuple(updated)

    summed = lax.fori_loop(0, piece_blocks.shape[0], visit, tuple(totals))
    attended = summed[0]
    centre = jnp.mean(attended, -1, keepdims=True)
    shifted = attended - centre
    inv_std = lax.rsqrt(jnp.mean(shifted * shifted, -1, keepdims=True) + 1e-05)
    normed = shifted * inv_std
    gates_f = gates.astype(jnp.float32)
    mixed = (normed * gates_f).astype(jnp.bfloat16)
    weights_row = ips_weight[0]
    items = item_ids[0]
    fresh = jnp.concatenate(
        [(items[1:] != items[:-1]).astype(jnp.float32), jnp.zeros((1,), jnp.float32)]
    )
    scaled = weights_row * fresh * weights_row.shape[0] / jnp.sum(weights_row)
    local_scale = lax.dynamic_slice_in_dim(scaled, ctx_rank * count, count)
    grad_mixed = local_scale[:, None, None] * upstream[0].astype(jnp.float32)
    grad_gates = (grad_mixed * normed).astype(jnp.bfloat16)
    grad_normed = grad_mixed * gates_f
    grad_att = inv_std * (
        grad_normed
        - jnp.mean(grad_normed, -1, keepdims=True)
        - normed * jnp.mean(grad_normed * normed, -1, keepdims=True)
    )
    grad_flat = grad_att.astype(jnp.bfloat16)
    grad_rows = grad_flat.reshape(local_blocks, block, heads, width)
    grad_q = []
    grad_kv = []
    local = 0
    current = pair_blocks[local]
    own_q, own_k, own_v = attend_back(
        queries[local], grad_rows[local], current[:, :, 0], current[:, :, 1], own_masks[local]
    )
    near_q, near_k, near_v = attend_back(
        queries[local],
        grad_rows[local],
        prior[local][:, :, 0],
        prior[local][:, :, 1],
        prev_masks[local],
    )
    grad_q.append(own_q + near_q)
    grad_kv.append(jnp.stack([own_k, own_v], 2))
    backward_prev = jnp.stack([near_k, near_v], 2)
    incoming = shifted_2(backward_prev.astype(jnp.bfloat16), "ctx", -1).astype(jnp.float32)
    grad_kv[local_blocks - 1] = grad_kv[local_blocks - 1] + incoming
    pulled = jnp.stack([rows[:, :, 1], grad_flat], 2)
    piece_pairs = lax.all_gather(pairs, "ctx", axis=0, tiled=True).reshape(
        -1, block, heads, 2, width
    )
    piece_pulled = lax.all_gather(pulled, "ctx", axis=0, tiled=True).reshape(
        -1, block, heads, 2, width
    )

    def visit(index, acc):
        sums, owned = acc
        chosen = lax.dynamic_index_in_dim(piece_pairs, index, 0, keepdims=False)
        asked = lax.dynamic_index_in_dim(piece_pulled, index, 0, keepdims=False)
        target_list = lax.dynamic_index_in_dim(lists, index, 0, keepdims=False)
        local = 0
        hit = jnp.any(list_rows[local] == index)
        new_sums = [
            lax.cond(
                hit,
                lambda value, local=local: value
                + attend_back(
                    queries[local], grad_rows[local], chosen[:, :, 0], chosen[:, :, 1], everything
                )[0],
                lambda value: value,
                sums[local],
            )
        ]
        mine = jnp.any(target_list == first + local)

        def owner_add(value, local=local):
            part_q, part_k, part_v = attend_back(
                asked[:, :, 0],
                asked[:, :, 1],
                pair_blocks[local][:, :, 0],
                pair_blocks[local][:, :, 1],
                everything,
            )
            return value + jnp.stack([part_k, part_v], 2)

        new_owned = [lax.cond(mine, owner_add, lambda value: value, owned[local])]
        return (tuple(new_sums), tuple(new_owned))

    sums, owned = lax.fori_loop(0, piece_pairs.shape[0], visit, (tuple(grad_q), tuple(grad_kv)))
    grad_q = list(sums)
    grad_kv = list(owned)
    grad_q_all = grad_q[0].astype(jnp.bfloat16)
    grad_kv_all = grad_kv[0].astype(jnp.bfloat16)
    result = jnp.concatenate([grad_gates[:, :, None], grad_q_all[:, :, None], grad_kv_all], 2)
    return (mixed[None], result[None])


MESH = pl.DeviceIdType.MESH
NT = (((1,), (1,)), ((), ()))
TN = (((0,), (0,)), ((), ()))
NN = (((1,), (0,)), ((), ()))


def dot(a, b, dims):
    return lax.dot_general(a, b, dims, preferred_element_type=jnp.float32)


def four_kernel(
    heads,
    proj,
    up,
    cvec,
    sess_row,
    sess_col,
    listed,
    mixed,
    grads,
    qb,
    kb,
    gb,
    yin,
    yout,
    dqin,
    dqout,
    dkvin,
    dkvout,
    ptab,
    stab,
    mask,
    yown,
    acc,
    dkv,
    dkvown,
    q_sem,
    y_sem,
    g_sem,
    dq_sem,
    kv_sem,
    dkv_sem,
):
    me = lax.axis_index("ctx")
    block, width = up.shape[1], up.shape[2]
    scale = width ** (-0.5)
    half = block // 2
    n_q = jnp.where(me == 1, 3, jnp.where(me == 2, 2, 1))
    n_kv = jnp.where(me == 1, 2, 1)

    barrier = pltpu.get_barrier_semaphore()
    for d in range(1, 4):
        pl.semaphore_signal(
            barrier, inc=1, device_id={"ctx": lax.rem(me + d, 4)}, device_id_type=MESH
        )
    pl.semaphore_wait(barrier, 3)

    def remote(src, dst, sem, slot, h, to):
        return pltpu.make_async_remote_copy(
            src_ref=src,
            dst_ref=dst,
            send_sem=sem.at[0, slot, h],
            recv_sem=sem.at[1, slot, h],
            device_id={"ctx": to},
            device_id_type=MESH,
        )

    def q_copy(d, h):
        return remote(proj.at[h, 1], qb.at[d, h], q_sem, d - 1, h, lax.rem(me + 4 - d, 4))

    def g_copy(d, h):
        return remote(gb.at[0, h], gb.at[d, h], g_sem, d - 1, h, lax.rem(me + 4 - d, 4))

    def y_copy(d, h):
        return remote(yout.at[d - 1, h], yin.at[d - 1, h], y_sem, d - 1, h, lax.rem(me + d, 4))

    def dq_copy(d, h):
        return remote(dqout.at[d - 1, h], dqin.at[d - 1, h], dq_sem, d - 1, h, lax.rem(me + d, 4))

    def kv_copy(h):
        return remote(proj.at[h, pl.ds(2, 2)], kb.at[1, h], kv_sem, 0, h, lax.rem(me + 1, 4))

    def dkv_copy(h):
        return remote(dkvout.at[h], dkvin.at[h], dkv_sem, 0, h, lax.rem(me + 3, 4))

    asks = {1: me >= 2, 2: me == 3}
    helps = {1: (me == 1) | (me == 2), 2: me == 1}

    for h in range(heads):
        for d in (2, 1):

            @pl.when(asks[d])
            def _():
                q_copy(d, h).start()

        @pl.when(me == 0)
        def _():
            kv_copy(h).start()

    qb[0] = proj[:, 1]
    kb[0] = proj[:, 2:4]

    def fill(pair, carry):
        qi, kj = pair // 2, lax.rem(pair, 2)

        @pl.when((qi < n_q) & (kj < n_kv))
        def _():
            bq, bk = me + qi, me - kj
            row = sess_row[bq]
            gap = bq - bk
            full = listed[bq * 4 + bk]
            for t in range(2):
                col = sess_col[bk, pl.ds(t * half, half)]
                c = lax.broadcasted_iota(jnp.int32, (half, block), 0) + t * half
                a = lax.broadcasted_iota(jnp.int32, (half, block), 1)
                ahead = a - c + gap * block
                window = (ahead >= 0) & (ahead < block)
                near = jnp.where(window & (row == col), 1.0, 0.0)
                mask[pair, pl.ds(t * half, half)] = jnp.maximum(near, full)

        return carry

    lax.fori_loop(0, 6, fill, 0)

    def forward(h, carry):
        @pl.when(me == 1)
        def _():
            kv_copy(h).wait_recv()

        def one_q(qi, carry):
            for d in (1, 2):

                @pl.when((qi == d) & helps[d])
                def _():
                    q_copy(d, h).wait_recv()

            acc[...] = jnp.zeros_like(acc)
            query = qb[qi, h]

            def one_k(kj, carry):
                pair = qi * 2 + kj
                for t in range(2):
                    part = pl.ds(t * half, half)
                    raw = dot(kb[kj, h, 0, part], query, NT)
                    sigma = 0.5 * jnp.tanh(raw * (0.5 * scale)) + 0.5
                    prob = raw * scale * sigma
                    slope = sigma + prob * (1.0 - sigma)
                    seen = mask[pair, part]
                    prob = (prob * seen).astype(jnp.bfloat16)
                    ptab[pair, h, part] = prob
                    stab[pair, h, part] = (slope * seen).astype(jnp.bfloat16)
                    acc[...] += dot(kb[kj, h, 1, part], prob, TN)
                return carry

            lax.fori_loop(0, n_kv, one_k, 0)

            @pl.when(qi == 0)
            def _():
                yown[h] = acc[...].T

            for d in (1, 2):

                @pl.when((qi == d) & helps[d])
                def _():
                    yout[d - 1, h] = acc[...].T.astype(jnp.bfloat16)
                    y_copy(d, h).start()

            return carry

        return lax.fori_loop(0, n_q, one_q, carry)

    lax.fori_loop(0, heads, forward, 0)

    def norm(h, carry):
        for d in (1, 2):

            @pl.when(asks[d])
            def _():
                y_copy(d, h).wait_recv()
                yown[h] = yown[h] + yin[d - 1, h].astype(jnp.float32)

        y = yown[h]
        centre = jnp.mean(y, -1, keepdims=True)
        shifted = y - centre
        inv_std = lax.rsqrt(jnp.mean(shifted * shifted, -1, keepdims=True) + 1e-05)
        normed = shifted * inv_std
        gate = proj[h, 0].astype(jnp.float32)
        mixed[h] = (normed * gate).astype(jnp.bfloat16)
        grad_mixed = cvec[...] * up[h].astype(jnp.float32)
        grads[h, 0] = (grad_mixed * normed).astype(jnp.bfloat16)
        grad_normed = grad_mixed * gate
        grad_att = inv_std * (
            grad_normed
            - jnp.mean(grad_normed, -1, keepdims=True)
            - normed * jnp.mean(grad_normed * normed, -1, keepdims=True)
        )
        gb[0, h] = grad_att.astype(jnp.bfloat16)
        for d in (2, 1):

            @pl.when(asks[d])
            def _():
                g_copy(d, h).start()

        return carry

    lax.fori_loop(0, heads, norm, 0)

    def backward(h, carry):
        dkv[...] = jnp.zeros_like(dkv)

        def one_q(qi, carry):
            for d in (1, 2):

                @pl.when((qi == d) & helps[d])
                def _():
                    g_copy(d, h).wait_recv()

            acc[...] = jnp.zeros_like(acc)
            query = qb[qi, h]
            grad = gb[qi, h]

            def one_k(kj, carry):
                pair = qi * 2 + kj
                for t in range(2):
                    part = pl.ds(t * half, half)
                    dprod = dot(kb[kj, h, 1, part], grad, NT)
                    edge = (dprod * stab[pair, h, part].astype(jnp.float32)).astype(jnp.bfloat16)
                    acc[...] += dot(kb[kj, h, 0, part], edge, TN)
                    dkv[kj, 0, part] += dot(edge, query, NN)
                    dkv[kj, 1, part] += dot(ptab[pair, h, part], grad, NN)
                return carry

            lax.fori_loop(0, n_kv, one_k, 0)

            @pl.when(qi == 0)
            def _():
                yown[h] = acc[...].T * scale

            for d in (1, 2):

                @pl.when((qi == d) & helps[d])
                def _():
                    dqout[d - 1, h] = (acc[...].T * scale).astype(jnp.bfloat16)
                    dq_copy(d, h).start()

            return carry

        lax.fori_loop(0, n_q, one_q, 0)

        @pl.when(me == 1)
        def _():
            dkvout[h, 0] = (dkv[1, 0] * scale).astype(jnp.bfloat16)
            dkvout[h, 1] = dkv[1, 1].astype(jnp.bfloat16)
            dkv_copy(h).start()

        dkvown[h, 0] = dkv[0, 0] * scale
        dkvown[h, 1] = dkv[0, 1]
        return carry

    lax.fori_loop(0, heads, backward, 0)

    def finish(h, carry):
        for d in (1, 2):

            @pl.when(asks[d])
            def _():
                dq_copy(d, h).wait_recv()
                yown[h] = yown[h] + dqin[d - 1, h].astype(jnp.float32)

        @pl.when(me == 0)
        def _():
            dkv_copy(h).wait_recv()
            dkvown[h] = dkvown[h] + dkvin[h].astype(jnp.float32)

        grads[h, 1] = yown[h].astype(jnp.bfloat16)
        grads[h, 2:4] = dkvown[h].astype(jnp.bfloat16)
        return carry

    lax.fori_loop(0, heads, finish, 0)

    def drain(h, carry):
        for d in (1, 2):

            @pl.when(asks[d])
            def _():
                q_copy(d, h).wait_send()
                g_copy(d, h).wait_send()

            @pl.when(helps[d])
            def _():
                y_copy(d, h).wait_send()
                dq_copy(d, h).wait_send()

        @pl.when(me == 0)
        def _():
            kv_copy(h).wait_send()

        @pl.when(me == 1)
        def _():
            dkv_copy(h).wait_send()

        return carry

    lax.fori_loop(0, heads, drain, 0)


def four_shards(projected, upstream, ips_weight, item_ids, session_ids, session_blocks):
    rows = projected[0]
    count, heads, _, width = rows.shape
    ctx_rank = lax.axis_index("ctx")
    proj = jnp.transpose(rows, (1, 2, 0, 3))
    up = jnp.transpose(upstream[0], (1, 0, 2))
    weights_row = ips_weight[0]
    items = item_ids[0]
    fresh = jnp.concatenate(
        [(items[1:] != items[:-1]).astype(jnp.float32), jnp.zeros((1,), jnp.float32)]
    )
    scaled = weights_row * fresh * weights_row.shape[0] / jnp.sum(weights_row)
    cvec = lax.dynamic_slice_in_dim(scaled, ctx_rank * count, count)[:, None]
    lists = session_blocks[0]
    total = lists.shape[0]
    listed = jnp.any(lists[:, :, None] == jnp.arange(total)[None, None, :], 1)
    listed = jnp.broadcast_to(
        listed.astype(jnp.float32).reshape(total * total, 1, 1), (total * total, 1, count)
    )
    sess_row = session_ids[0].reshape(total, 1, count)
    sess_col = session_ids[0].reshape(total, count, 1)
    bf, f32 = jnp.bfloat16, jnp.float32
    vmem = pl.BlockSpec(memory_space=pltpu.VMEM)
    piece = (heads, count, width)
    sems = pltpu.SemaphoreType.DMA
    mixed, grads = pl.pallas_call(
        functools.partial(four_kernel, heads),
        out_shape=(
            jax.ShapeDtypeStruct(piece, bf),
            jax.ShapeDtypeStruct((heads, 4, count, width), bf),
        ),
        in_specs=[vmem] * 6,
        out_specs=(vmem, vmem),
        scratch_shapes=[
            pltpu.VMEM((3,) + piece, bf),
            pltpu.VMEM((2, heads, 2, count, width), bf),
            pltpu.VMEM((3,) + piece, bf),
            pltpu.VMEM((2,) + piece, bf),
            pltpu.VMEM((2,) + piece, bf),
            pltpu.VMEM((2,) + piece, bf),
            pltpu.VMEM((2,) + piece, bf),
            pltpu.VMEM((heads, 2, count, width), bf),
            pltpu.VMEM((heads, 2, count, width), bf),
            pltpu.VMEM((6, heads, count, count), bf),
            pltpu.VMEM((6, heads, count, count), bf),
            pltpu.VMEM((6, count, count), f32),
            pltpu.VMEM(piece, f32),
            pltpu.VMEM((width, count), f32),
            pltpu.VMEM((2, 2, count, width), f32),
            pltpu.VMEM((heads, 2, count, width), f32),
            sems((2, 2, heads)),
            sems((2, 2, heads)),
            sems((2, 2, heads)),
            sems((2, 2, heads)),
            sems((2, 1, heads)),
            sems((2, 1, heads)),
        ],
        compiler_params=pltpu.CompilerParams(
            collective_id=0, has_side_effects=True, vmem_limit_bytes=60 * 1024 * 1024
        ),
    )(proj, up, cvec, sess_row, sess_col, listed)
    mixed = jnp.transpose(mixed, (1, 0, 2))
    grads = jnp.transpose(grads, (2, 0, 1, 3))
    return (mixed[None], grads[None])


def solution(mesh):
    body = four_shards if mesh.shape["ctx"] == 4 else shards
    placed = (
        P(("groups", "user"), "ctx", "head", None, None),
        P(("groups", "user"), "ctx", "head", None),
        P(("groups", "user"), None),
        P(("groups", "user"), None),
        P(("groups", "user"), None),
        P(("groups", "user"), None, None),
    )
    return jax.shard_map(
        body,
        mesh=mesh,
        in_specs=placed,
        out_specs=(
            P(("groups", "user"), "ctx", "head", None),
            P(("groups", "user"), "ctx", "head", None, None),
        ),
        check_vma=False,
    )
```

```python
import functools
import jax
import jax.numpy as jnp
from jax import lax
from jax.experimental import pallas as pl
from jax.experimental.pallas import tpu as pltpu
from jax.sharding import PartitionSpec as P

BLOCK = 512


def shifted_2(block, axis, distance):
    devices = range(lax.axis_size(axis))
    route = [(i - distance, i) for i in devices if i - distance in devices]
    return lax.ppermute(block, axis, route)


def pair_scores(queries, keys):
    scale = queries.shape[-1] ** (-0.5)
    return jnp.einsum("ahd,chd->hac", queries, keys, preferred_element_type=jnp.float32) * scale


def attend(queries, keys, values, visible):
    scores = pair_scores(queries, keys)
    probs = jnp.where(visible[None], jax.nn.silu(scores), 0.0).astype(jnp.bfloat16)
    return jnp.einsum("hac,chd->ahd", probs, values, preferred_element_type=jnp.float32)


def attend_back(queries, grad_rows, keys, values, visible):
    scale = queries.shape[-1] ** (-0.5)
    scores = pair_scores(queries, keys)
    sigma = jax.nn.sigmoid(scores)
    probs = jnp.where(visible[None], jax.nn.silu(scores), 0.0).astype(jnp.bfloat16)
    slope = sigma * (1.0 + scores * (1.0 - sigma))
    dprod = jnp.einsum("ahd,chd->hac", grad_rows, values, preferred_element_type=jnp.float32)
    edges = jnp.where(visible[None], dprod * slope, 0.0).astype(jnp.bfloat16)
    grad_q = jnp.einsum("hac,chd->ahd", edges, keys, preferred_element_type=jnp.float32) * scale
    grad_k = jnp.einsum("hac,ahd->chd", edges, queries, preferred_element_type=jnp.float32) * scale
    grad_v = jnp.einsum("hac,ahd->chd", probs, grad_rows, preferred_element_type=jnp.float32)
    return (grad_q, grad_k, grad_v)


def shards(projected, upstream, ips_weight, item_ids, session_ids, session_blocks):
    rows = projected[0]
    count = rows.shape[0]
    heads = rows.shape[1]
    width = rows.shape[3]
    block = BLOCK
    local_blocks = count // block
    ctx_rank = lax.axis_index("ctx")
    first = ctx_rank * local_blocks
    sessions = session_ids[0]
    lists = session_blocks[0]
    gates = rows[:, :, 0]
    queries = rows[:, :, 1].reshape(local_blocks, block, heads, width)
    pairs = rows[:, :, 2:4]
    pair_blocks = pairs.reshape(local_blocks, block, heads, 2, width)
    inner = jnp.arange(block)
    below = inner[None, :] <= inner[:, None]
    everything = jnp.ones((block, block), bool)

    def session_slice(index):
        return lax.dynamic_slice_in_dim(sessions, jnp.maximum(index, 0) * block, block)

    list_rows = []
    local = 0
    glob = first + local
    here = session_slice(glob)
    there = session_slice(glob - 1)
    list_row = lax.dynamic_index_in_dim(lists, glob, 0, keepdims=False)
    prev_listed = jnp.any(list_row == glob - 1)
    own_masks = [below & (here[:, None] == here[None, :])]
    prev_masks = [
        jnp.logical_not(below)
        & (here[:, None] == there[None, :])
        & (glob > 0)
        & jnp.logical_not(prev_listed)
    ]
    list_rows.append(list_row)
    previous = shifted_2(pair_blocks[local_blocks - 1], "ctx", 1)
    prior = [previous] + [pair_blocks[local] for local in range(local_blocks - 1)]
    local = 0
    current = pair_blocks[local]
    total = attend(queries[local], current[:, :, 0], current[:, :, 1], own_masks[local])
    total = total + attend(
        queries[local], prior[local][:, :, 0], prior[local][:, :, 1], prev_masks[local]
    )
    totals = [total]
    piece_blocks = lax.all_gather(pairs, "ctx", axis=0, tiled=True).reshape(
        -1, block, heads, 2, width
    )

    def visit(index, acc):
        chosen = lax.dynamic_index_in_dim(piece_blocks, index, 0, keepdims=False)
        local = 0
        hit = jnp.any(list_rows[local] == index)
        updated = [
            lax.cond(
                hit,
                lambda value, local=local: value
                + attend(queries[local], chosen[:, :, 0], chosen[:, :, 1], everything),
                lambda value: value,
                acc[local],
            )
        ]
        return tuple(updated)

    summed = lax.fori_loop(0, piece_blocks.shape[0], visit, tuple(totals))
    attended = summed[0]
    centre = jnp.mean(attended, -1, keepdims=True)
    shifted = attended - centre
    inv_std = lax.rsqrt(jnp.mean(shifted * shifted, -1, keepdims=True) + 1e-05)
    normed = shifted * inv_std
    gates_f = gates.astype(jnp.float32)
    mixed = (normed * gates_f).astype(jnp.bfloat16)
    weights_row = ips_weight[0]
    items = item_ids[0]
    fresh = jnp.concatenate(
        [(items[1:] != items[:-1]).astype(jnp.float32), jnp.zeros((1,), jnp.float32)]
    )
    scaled = weights_row * fresh * weights_row.shape[0] / jnp.sum(weights_row)
    local_scale = lax.dynamic_slice_in_dim(scaled, ctx_rank * count, count)
    grad_mixed = local_scale[:, None, None] * upstream[0].astype(jnp.float32)
    grad_gates = (grad_mixed * normed).astype(jnp.bfloat16)
    grad_normed = grad_mixed * gates_f
    grad_att = inv_std * (
        grad_normed
        - jnp.mean(grad_normed, -1, keepdims=True)
        - normed * jnp.mean(grad_normed * normed, -1, keepdims=True)
    )
    grad_flat = grad_att.astype(jnp.bfloat16)
    grad_rows = grad_flat.reshape(local_blocks, block, heads, width)
    grad_q = []
    grad_kv = []
    local = 0
    current = pair_blocks[local]
    own_q, own_k, own_v = attend_back(
        queries[local], grad_rows[local], current[:, :, 0], current[:, :, 1], own_masks[local]
    )
    near_q, near_k, near_v = attend_back(
        queries[local],
        grad_rows[local],
        prior[local][:, :, 0],
        prior[local][:, :, 1],
        prev_masks[local],
    )
    grad_q.append(own_q + near_q)
    grad_kv.append(jnp.stack([own_k, own_v], 2))
    backward_prev = jnp.stack([near_k, near_v], 2)
    incoming = shifted_2(backward_prev.astype(jnp.bfloat16), "ctx", -1).astype(jnp.float32)
    grad_kv[local_blocks - 1] = grad_kv[local_blocks - 1] + incoming
    pulled = jnp.stack([rows[:, :, 1], grad_flat], 2)
    piece_pairs = lax.all_gather(pairs, "ctx", axis=0, tiled=True).reshape(
        -1, block, heads, 2, width
    )
    piece_pulled = lax.all_gather(pulled, "ctx", axis=0, tiled=True).reshape(
        -1, block, heads, 2, width
    )

    def visit(index, acc):
        sums, owned = acc
        chosen = lax.dynamic_index_in_dim(piece_pairs, index, 0, keepdims=False)
        asked = lax.dynamic_index_in_dim(piece_pulled, index, 0, keepdims=False)
        target_list = lax.dynamic_index_in_dim(lists, index, 0, keepdims=False)
        local = 0
        hit = jnp.any(list_rows[local] == index)
        new_sums = [
            lax.cond(
                hit,
                lambda value, local=local: value
                + attend_back(
                    queries[local], grad_rows[local], chosen[:, :, 0], chosen[:, :, 1], everything
                )[0],
                lambda value: value,
                sums[local],
            )
        ]
        mine = jnp.any(target_list == first + local)

        def owner_add(value, local=local):
            part_q, part_k, part_v = attend_back(
                asked[:, :, 0],
                asked[:, :, 1],
                pair_blocks[local][:, :, 0],
                pair_blocks[local][:, :, 1],
                everything,
            )
            return value + jnp.stack([part_k, part_v], 2)

        new_owned = [lax.cond(mine, owner_add, lambda value: value, owned[local])]
        return (tuple(new_sums), tuple(new_owned))

    sums, owned = lax.fori_loop(0, piece_pairs.shape[0], visit, (tuple(grad_q), tuple(grad_kv)))
    grad_q = list(sums)
    grad_kv = list(owned)
    grad_q_all = grad_q[0].astype(jnp.bfloat16)
    grad_kv_all = grad_kv[0].astype(jnp.bfloat16)
    result = jnp.concatenate([grad_gates[:, :, None], grad_q_all[:, :, None], grad_kv_all], 2)
    return (mixed[None], result[None])


MESH = pl.DeviceIdType.MESH
NT = (((1,), (1,)), ((), ()))
TN = (((0,), (0,)), ((), ()))
NN = (((1,), (0,)), ((), ()))


def dot(a, b, dims):
    return lax.dot_general(a, b, dims, preferred_element_type=jnp.float32)


def four_kernel(
    heads,
    proj,
    up,
    weights,
    items,
    sessions,
    lists,
    mixed,
    grads,
    qb,
    kb,
    gb,
    yin,
    yout,
    dqin,
    dqout,
    dkvin,
    dkvout,
    ptab,
    stab,
    mask,
    yown,
    acc,
    dkv,
    dkvown,
    rowbuf,
    cmat,
    q_sem,
    y_sem,
    g_sem,
    dq_sem,
    kv_sem,
    dkv_sem,
):
    me = lax.axis_index("ctx")
    block, width = up.shape[1], up.shape[2]
    total = weights.shape[1]
    scale = width ** (-0.5)
    chunks = 2
    step = block // chunks

    def odd(h):
        return lax.rem(jnp.int32(h), jnp.int32(2)) == 1

    def n_q(h):
        return jnp.where(me == 2, 2, jnp.where((me == 1) & jnp.logical_not(odd(h)), 3, 1))

    def n_kv(h):
        return jnp.where(me == 1, 2, jnp.where((me == 2) & odd(h), 3, 1))

    def helps(d, h):
        return n_q(h) > d

    def asks(d, h):
        return jnp.where(odd(h), me == 3 if d == 1 else me > 3, me >= d + 1)

    def takes(d, h):
        return n_kv(h) > d

    def gives(d, h):
        return jnp.where(odd(h), me <= 2 - d, me == 0 if d == 1 else me < 0)

    max_q = jnp.where(me == 1, 3, jnp.where(me == 2, 2, 1))
    max_kv = jnp.where(me == 1, 2, jnp.where(me == 2, 3, 1))

    barrier = pltpu.get_barrier_semaphore()
    for d in range(1, 4):
        pl.semaphore_signal(
            barrier, inc=1, device_id={"ctx": lax.rem(me + d, 4)}, device_id_type=MESH
        )
    pl.semaphore_wait(barrier, 3)

    def remote(src, dst, sem, slot, h, to):
        return pltpu.make_async_remote_copy(
            src_ref=src,
            dst_ref=dst,
            send_sem=sem.at[0, slot, h],
            recv_sem=sem.at[1, slot, h],
            device_id={"ctx": to},
            device_id_type=MESH,
        )

    def q_copy(d, h):
        return remote(proj.at[h, 1], qb.at[d, h], q_sem, d - 1, h, lax.rem(me + 4 - d, 4))

    def g_copy(d, h):
        return remote(gb.at[0, h], gb.at[d, h], g_sem, d - 1, h, lax.rem(me + 4 - d, 4))

    def y_copy(d, h):
        return remote(yout.at[d - 1, h], yin.at[d - 1, h], y_sem, d - 1, h, lax.rem(me + d, 4))

    def dq_copy(d, h):
        return remote(dqout.at[d - 1, h], dqin.at[d - 1, h], dq_sem, d - 1, h, lax.rem(me + d, 4))

    def kv_copy(d, h):
        return remote(
            proj.at[h, pl.ds(2, 2)], kb.at[d, h], kv_sem, d - 1, h, lax.rem(me + d, 4)
        )

    def dkv_copy(d, h):
        return remote(
            dkvout.at[d - 1, h], dkvin.at[d - 1, h], dkv_sem, d - 1, h, lax.rem(me + 4 - d, 4)
        )

    for h in range(heads):
        for d in (2, 1):

            @pl.when(asks(d, h))
            def _():
                q_copy(d, h).start()

            @pl.when(gives(d, h))
            def _():
                kv_copy(d, h).start()

    qb[0] = proj[:, 1]
    kb[0] = proj[:, 2:4]

    def run_row(source, index):
        rowbuf[0:1] = source
        return rowbuf[0:1, pl.ds(pl.multiple_of(index * block, block), block)]

    def down(row):
        return jnp.broadcast_to(row, (width, block)).T

    ids = items[...]
    place = lax.broadcasted_iota(jnp.int32, (1, total), 1)
    fresh = (pltpu.roll(ids, total - 1, 1) != ids) & (place < total - 1)
    loss = weights[...]
    loss = loss * jnp.where(fresh, 1.0, 0.0) * total / jnp.sum(loss)
    cmat[...] = down(run_row(loss, me))

    def fill(pair, carry):
        qi, kj = pair // max_kv, lax.rem(pair, max_kv)
        bq, bk = me + qi, me - kj
        row = run_row(sessions[...].astype(jnp.float32), bq)
        col = down(run_row(sessions[...].astype(jnp.float32), bk))
        col = jnp.concatenate([col] * (block // width), 1)
        full = jnp.float32(0.0)
        for slot in range(lists.shape[0]):
            full = jnp.maximum(full, jnp.where(lists[slot, 0, bq] == bk, 1.0, 0.0))
        c = lax.broadcasted_iota(jnp.int32, (block, block), 0)
        a = lax.broadcasted_iota(jnp.int32, (block, block), 1)
        ahead = a - c + (bq - bk) * block
        window = (ahead >= 0) & (ahead < block)
        near = jnp.where(window & (row == col), 1.0, 0.0)
        mask[pair] = jnp.maximum(near, full).astype(jnp.bfloat16)
        return carry

    lax.fori_loop(0, max_q * max_kv, fill, 0)

    def forward(h, carry):
        for d in (1, 2):

            @pl.when(takes(d, h))
            def _():
                kv_copy(d, h).wait_recv()

        def one_q(qi, carry):
            for d in (1, 2):

                @pl.when((qi == d) & helps(d, h))
                def _():
                    q_copy(d, h).wait_recv()

            acc[...] = jnp.zeros_like(acc)
            query = qb[qi, h]

            def one_k(kj, carry):
                pair = qi * n_kv(h) + kj
                for t in range(chunks):
                    part = pl.ds(t * step, step)
                    raw = dot(kb[kj, h, 0, part], query, NT)
                    sigma = 0.5 * jnp.tanh(raw * (0.5 * scale)) + 0.5
                    prob = raw * scale * sigma
                    slope = sigma + prob * (1.0 - sigma)
                    seen = mask[qi * max_kv + kj, part]
                    prob = prob.astype(jnp.bfloat16) * seen
                    ptab[pair, h, part] = prob
                    stab[pair, h, part] = slope.astype(jnp.bfloat16) * seen
                    acc[...] += dot(kb[kj, h, 1, part], prob, TN)
                return carry

            lax.fori_loop(0, n_kv(h), one_k, 0)

            @pl.when(qi == 0)
            def _():
                yown[h] = acc[...].T

            for d in (1, 2):

                @pl.when((qi == d) & helps(d, h))
                def _():
                    yout[d - 1, h] = acc[...].T.astype(jnp.bfloat16)
                    y_copy(d, h).start()

            return carry

        return lax.fori_loop(0, n_q(h), one_q, carry)

    lax.fori_loop(0, heads, forward, 0)

    def norm(h, carry):
        for d in (1, 2):

            @pl.when(asks(d, h))
            def _():
                y_copy(d, h).wait_recv()
                yown[h] = yown[h] + yin[d - 1, h].astype(jnp.float32)

        y = yown[h]
        centre = jnp.mean(y, -1, keepdims=True)
        shifted = y - centre
        inv_std = lax.rsqrt(jnp.mean(shifted * shifted, -1, keepdims=True) + 1e-05)
        normed = shifted * inv_std
        gate = proj[h, 0].astype(jnp.float32)
        mixed[h] = (normed * gate).astype(jnp.bfloat16)
        grad_mixed = cmat[...] * up[h].astype(jnp.float32)
        grads[h, 0] = (grad_mixed * normed).astype(jnp.bfloat16)
        grad_normed = grad_mixed * gate
        grad_att = inv_std * (
            grad_normed
            - jnp.mean(grad_normed, -1, keepdims=True)
            - normed * jnp.mean(grad_normed * normed, -1, keepdims=True)
        )
        gb[0, h] = grad_att.astype(jnp.bfloat16)
        for d in (2, 1):

            @pl.when(asks(d, h))
            def _():
                g_copy(d, h).start()

        return carry

    lax.fori_loop(0, heads, norm, 0)

    def backward(h, carry):
        dkv[...] = jnp.zeros_like(dkv)

        def one_q(qi, carry):
            for d in (1, 2):

                @pl.when((qi == d) & helps(d, h))
                def _():
                    g_copy(d, h).wait_recv()

            acc[...] = jnp.zeros_like(acc)
            query = qb[qi, h]
            grad = gb[qi, h]

            def one_k(kj, carry):
                pair = qi * n_kv(h) + kj
                for t in range(chunks):
                    part = pl.ds(t * step, step)
                    dprod = dot(kb[kj, h, 1, part], grad, NT)
                    edge = (dprod * stab[pair, h, part].astype(jnp.float32)).astype(jnp.bfloat16)
                    acc[...] += dot(kb[kj, h, 0, part], edge, TN)
                    dkv[kj, 0, part] += dot(edge, query, NN)
                    dkv[kj, 1, part] += dot(ptab[pair, h, part], grad, NN)
                return carry

            lax.fori_loop(0, n_kv(h), one_k, 0)

            @pl.when(qi == 0)
            def _():
                yown[h] = acc[...].T * scale

            for d in (1, 2):

                @pl.when((qi == d) & helps(d, h))
                def _():
                    dqout[d - 1, h] = (acc[...].T * scale).astype(jnp.bfloat16)
                    dq_copy(d, h).start()

            return carry

        lax.fori_loop(0, n_q(h), one_q, 0)

        for d in (2, 1):

            @pl.when(takes(d, h))
            def _():
                dkvout[d - 1, h, 0] = (dkv[d, 0] * scale).astype(jnp.bfloat16)
                dkvout[d - 1, h, 1] = dkv[d, 1].astype(jnp.bfloat16)
                dkv_copy(d, h).start()

        dkvown[h, 0] = dkv[0, 0] * scale
        dkvown[h, 1] = dkv[0, 1]
        return carry

    lax.fori_loop(0, heads, backward, 0)

    def finish(h, carry):
        for d in (1, 2):

            @pl.when(asks(d, h))
            def _():
                dq_copy(d, h).wait_recv()
                yown[h] = yown[h] + dqin[d - 1, h].astype(jnp.float32)

            @pl.when(gives(d, h))
            def _():
                dkv_copy(d, h).wait_recv()
                dkvown[h] = dkvown[h] + dkvin[d - 1, h].astype(jnp.float32)

        grads[h, 1] = yown[h].astype(jnp.bfloat16)
        grads[h, 2:4] = dkvown[h].astype(jnp.bfloat16)
        return carry

    lax.fori_loop(0, heads, finish, 0)

    def drain(h, carry):
        for d in (1, 2):

            @pl.when(asks(d, h))
            def _():
                q_copy(d, h).wait_send()
                g_copy(d, h).wait_send()

            @pl.when(helps(d, h))
            def _():
                y_copy(d, h).wait_send()
                dq_copy(d, h).wait_send()

            @pl.when(gives(d, h))
            def _():
                kv_copy(d, h).wait_send()

            @pl.when(takes(d, h))
            def _():
                dkv_copy(d, h).wait_send()

        return carry

    lax.fori_loop(0, heads, drain, 0)


def four_shards(projected, upstream, ips_weight, item_ids, session_ids, session_blocks):
    rows = projected[0]
    count, heads, _, width = rows.shape
    proj = jnp.transpose(rows, (1, 2, 0, 3))
    up = jnp.transpose(upstream[0], (1, 0, 2))
    lists = jnp.transpose(session_blocks, (2, 0, 1))
    bf, f32 = jnp.bfloat16, jnp.float32
    vmem = pl.BlockSpec(memory_space=pltpu.VMEM)
    piece = (heads, count, width)
    sems = pltpu.SemaphoreType.DMA
    mixed, grads = pl.pallas_call(
        functools.partial(four_kernel, heads),
        out_shape=(
            jax.ShapeDtypeStruct(piece, bf),
            jax.ShapeDtypeStruct((heads, 4, count, width), bf),
        ),
        in_specs=[vmem] * 5 + [pl.BlockSpec(memory_space=pltpu.SMEM)],
        out_specs=(vmem, vmem),
        scratch_shapes=[
            pltpu.VMEM((3,) + piece, bf),
            pltpu.VMEM((3, heads, 2, count, width), bf),
            pltpu.VMEM((3,) + piece, bf),
            pltpu.VMEM((2,) + piece, bf),
            pltpu.VMEM((2,) + piece, bf),
            pltpu.VMEM((2,) + piece, bf),
            pltpu.VMEM((2,) + piece, bf),
            pltpu.VMEM((2, heads, 2, count, width), bf),
            pltpu.VMEM((2, heads, 2, count, width), bf),
            pltpu.VMEM((6, heads, count, count), bf),
            pltpu.VMEM((6, heads, count, count), bf),
            pltpu.VMEM((6, count, count), bf),
            pltpu.VMEM(piece, f32),
            pltpu.VMEM((width, count), f32),
            pltpu.VMEM((3, 2, count, width), f32),
            pltpu.VMEM((heads, 2, count, width), f32),
            pltpu.VMEM((8, ips_weight.shape[1]), f32),
            pltpu.VMEM((count, width), f32),
            sems((2, 2, heads)),
            sems((2, 2, heads)),
            sems((2, 2, heads)),
            sems((2, 2, heads)),
            sems((2, 2, heads)),
            sems((2, 2, heads)),
        ],
        compiler_params=pltpu.CompilerParams(
            collective_id=0, has_side_effects=True, vmem_limit_bytes=60 * 1024 * 1024
        ),
    )(proj, up, ips_weight, item_ids, session_ids, lists)
    mixed = jnp.transpose(mixed, (1, 0, 2))
    grads = jnp.transpose(grads, (2, 0, 1, 3))
    return (mixed[None], grads[None])


def solution(mesh):
    body = four_shards if mesh.shape["ctx"] == 4 else shards
    placed = (
        P(("groups", "user"), "ctx", "head", None, None),
        P(("groups", "user"), "ctx", "head", None),
        P(("groups", "user"), None),
        P(("groups", "user"), None),
        P(("groups", "user"), None),
        P(("groups", "user"), None, None),
    )
    return jax.shard_map(
        body,
        mesh=mesh,
        in_specs=placed,
        out_specs=(
            P(("groups", "user"), "ctx", "head", None),
            P(("groups", "user"), "ctx", "head", None, None),
        ),
        check_vma=False,
    )
```

```python
import functools
import jax
import jax.numpy as jnp
from jax import lax
from jax.experimental import pallas as pl
from jax.experimental.pallas import tpu as pltpu
from jax.sharding import PartitionSpec as P

BLOCK = 512


def shifted_2(block, axis, distance):
    devices = range(lax.axis_size(axis))
    route = [(i - distance, i) for i in devices if i - distance in devices]
    return lax.ppermute(block, axis, route)


def pair_scores(queries, keys):
    scale = queries.shape[-1] ** (-0.5)
    return jnp.einsum("ahd,chd->hac", queries, keys, preferred_element_type=jnp.float32) * scale


def attend(queries, keys, values, visible):
    scores = pair_scores(queries, keys)
    probs = jnp.where(visible[None], jax.nn.silu(scores), 0.0).astype(jnp.bfloat16)
    return jnp.einsum("hac,chd->ahd", probs, values, preferred_element_type=jnp.float32)


def attend_back(queries, grad_rows, keys, values, visible):
    scale = queries.shape[-1] ** (-0.5)
    scores = pair_scores(queries, keys)
    sigma = jax.nn.sigmoid(scores)
    probs = jnp.where(visible[None], jax.nn.silu(scores), 0.0).astype(jnp.bfloat16)
    slope = sigma * (1.0 + scores * (1.0 - sigma))
    dprod = jnp.einsum("ahd,chd->hac", grad_rows, values, preferred_element_type=jnp.float32)
    edges = jnp.where(visible[None], dprod * slope, 0.0).astype(jnp.bfloat16)
    grad_q = jnp.einsum("hac,chd->ahd", edges, keys, preferred_element_type=jnp.float32) * scale
    grad_k = jnp.einsum("hac,ahd->chd", edges, queries, preferred_element_type=jnp.float32) * scale
    grad_v = jnp.einsum("hac,ahd->chd", probs, grad_rows, preferred_element_type=jnp.float32)
    return (grad_q, grad_k, grad_v)


def shards(projected, upstream, ips_weight, item_ids, session_ids, session_blocks):
    rows = projected[0]
    count = rows.shape[0]
    heads = rows.shape[1]
    width = rows.shape[3]
    block = BLOCK
    local_blocks = count // block
    ctx_rank = lax.axis_index("ctx")
    first = ctx_rank * local_blocks
    sessions = session_ids[0]
    lists = session_blocks[0]
    gates = rows[:, :, 0]
    queries = rows[:, :, 1].reshape(local_blocks, block, heads, width)
    pairs = rows[:, :, 2:4]
    pair_blocks = pairs.reshape(local_blocks, block, heads, 2, width)
    inner = jnp.arange(block)
    below = inner[None, :] <= inner[:, None]
    everything = jnp.ones((block, block), bool)

    def session_slice(index):
        return lax.dynamic_slice_in_dim(sessions, jnp.maximum(index, 0) * block, block)

    list_rows = []
    local = 0
    glob = first + local
    here = session_slice(glob)
    there = session_slice(glob - 1)
    list_row = lax.dynamic_index_in_dim(lists, glob, 0, keepdims=False)
    prev_listed = jnp.any(list_row == glob - 1)
    own_masks = [below & (here[:, None] == here[None, :])]
    prev_masks = [
        jnp.logical_not(below)
        & (here[:, None] == there[None, :])
        & (glob > 0)
        & jnp.logical_not(prev_listed)
    ]
    list_rows.append(list_row)
    previous = shifted_2(pair_blocks[local_blocks - 1], "ctx", 1)
    prior = [previous] + [pair_blocks[local] for local in range(local_blocks - 1)]
    local = 0
    current = pair_blocks[local]
    total = attend(queries[local], current[:, :, 0], current[:, :, 1], own_masks[local])
    total = total + attend(
        queries[local], prior[local][:, :, 0], prior[local][:, :, 1], prev_masks[local]
    )
    totals = [total]
    piece_blocks = lax.all_gather(pairs, "ctx", axis=0, tiled=True).reshape(
        -1, block, heads, 2, width
    )

    def visit(index, acc):
        chosen = lax.dynamic_index_in_dim(piece_blocks, index, 0, keepdims=False)
        local = 0
        hit = jnp.any(list_rows[local] == index)
        updated = [
            lax.cond(
                hit,
                lambda value, local=local: value
                + attend(queries[local], chosen[:, :, 0], chosen[:, :, 1], everything),
                lambda value: value,
                acc[local],
            )
        ]
        return tuple(updated)

    summed = lax.fori_loop(0, piece_blocks.shape[0], visit, tuple(totals))
    attended = summed[0]
    centre = jnp.mean(attended, -1, keepdims=True)
    shifted = attended - centre
    inv_std = lax.rsqrt(jnp.mean(shifted * shifted, -1, keepdims=True) + 1e-05)
    normed = shifted * inv_std
    gates_f = gates.astype(jnp.float32)
    mixed = (normed * gates_f).astype(jnp.bfloat16)
    weights_row = ips_weight[0]
    items = item_ids[0]
    fresh = jnp.concatenate(
        [(items[1:] != items[:-1]).astype(jnp.float32), jnp.zeros((1,), jnp.float32)]
    )
    scaled = weights_row * fresh * weights_row.shape[0] / jnp.sum(weights_row)
    local_scale = lax.dynamic_slice_in_dim(scaled, ctx_rank * count, count)
    grad_mixed = local_scale[:, None, None] * upstream[0].astype(jnp.float32)
    grad_gates = (grad_mixed * normed).astype(jnp.bfloat16)
    grad_normed = grad_mixed * gates_f
    grad_att = inv_std * (
        grad_normed
        - jnp.mean(grad_normed, -1, keepdims=True)
        - normed * jnp.mean(grad_normed * normed, -1, keepdims=True)
    )
    grad_flat = grad_att.astype(jnp.bfloat16)
    grad_rows = grad_flat.reshape(local_blocks, block, heads, width)
    grad_q = []
    grad_kv = []
    local = 0
    current = pair_blocks[local]
    own_q, own_k, own_v = attend_back(
        queries[local], grad_rows[local], current[:, :, 0], current[:, :, 1], own_masks[local]
    )
    near_q, near_k, near_v = attend_back(
        queries[local],
        grad_rows[local],
        prior[local][:, :, 0],
        prior[local][:, :, 1],
        prev_masks[local],
    )
    grad_q.append(own_q + near_q)
    grad_kv.append(jnp.stack([own_k, own_v], 2))
    backward_prev = jnp.stack([near_k, near_v], 2)
    incoming = shifted_2(backward_prev.astype(jnp.bfloat16), "ctx", -1).astype(jnp.float32)
    grad_kv[local_blocks - 1] = grad_kv[local_blocks - 1] + incoming
    pulled = jnp.stack([rows[:, :, 1], grad_flat], 2)
    piece_pairs = lax.all_gather(pairs, "ctx", axis=0, tiled=True).reshape(
        -1, block, heads, 2, width
    )
    piece_pulled = lax.all_gather(pulled, "ctx", axis=0, tiled=True).reshape(
        -1, block, heads, 2, width
    )

    def visit(index, acc):
        sums, owned = acc
        chosen = lax.dynamic_index_in_dim(piece_pairs, index, 0, keepdims=False)
        asked = lax.dynamic_index_in_dim(piece_pulled, index, 0, keepdims=False)
        target_list = lax.dynamic_index_in_dim(lists, index, 0, keepdims=False)
        local = 0
        hit = jnp.any(list_rows[local] == index)
        new_sums = [
            lax.cond(
                hit,
                lambda value, local=local: value
                + attend_back(
                    queries[local], grad_rows[local], chosen[:, :, 0], chosen[:, :, 1], everything
                )[0],
                lambda value: value,
                sums[local],
            )
        ]
        mine = jnp.any(target_list == first + local)

        def owner_add(value, local=local):
            part_q, part_k, part_v = attend_back(
                asked[:, :, 0],
                asked[:, :, 1],
                pair_blocks[local][:, :, 0],
                pair_blocks[local][:, :, 1],
                everything,
            )
            return value + jnp.stack([part_k, part_v], 2)

        new_owned = [lax.cond(mine, owner_add, lambda value: value, owned[local])]
        return (tuple(new_sums), tuple(new_owned))

    sums, owned = lax.fori_loop(0, piece_pairs.shape[0], visit, (tuple(grad_q), tuple(grad_kv)))
    grad_q = list(sums)
    grad_kv = list(owned)
    grad_q_all = grad_q[0].astype(jnp.bfloat16)
    grad_kv_all = grad_kv[0].astype(jnp.bfloat16)
    result = jnp.concatenate([grad_gates[:, :, None], grad_q_all[:, :, None], grad_kv_all], 2)
    return (mixed[None], result[None])


MESH = pl.DeviceIdType.MESH
NT = (((1,), (1,)), ((), ()))
TN = (((0,), (0,)), ((), ()))
NN = (((1,), (0,)), ((), ()))


def dot(a, b, dims):
    return lax.dot_general(a, b, dims, preferred_element_type=jnp.float32)


def four_kernel(
    heads,
    proj,
    up,
    weights,
    items,
    sessions,
    lists,
    mixed,
    grads,
    qb,
    kb,
    gb,
    yin,
    yout,
    dqin,
    dqout,
    dkvin,
    dkvout,
    ptab,
    stab,
    mask,
    yown,
    acc,
    dkv,
    dkvown,
    rowbuf,
    cmat,
    edges,
    q_sem,
    y_sem,
    g_sem,
    dq_sem,
    kv_sem,
    dkv_sem,
):
    me = lax.axis_index("ctx")
    block, width = up.shape[1], up.shape[2]
    total = weights.shape[1]
    scale = width ** (-0.5)
    chunks = 2
    step = block // chunks

    n_q = jnp.where(me == 1, 3, jnp.where(me == 3, 1, 2))

    def n_kv(qi):
        return jnp.where((me == 1) & (qi > 0), 2, 1)

    asks = {1: me >= 1, 2: me == 3}
    helps = {1: me <= 2, 2: me == 1}

    barrier = pltpu.get_barrier_semaphore()
    for d in range(1, 4):
        pl.semaphore_signal(
            barrier, inc=1, device_id={"ctx": lax.rem(me + d, 4)}, device_id_type=MESH
        )
    pl.semaphore_wait(barrier, 3)

    def remote(src, dst, sem, slot, h, to):
        return pltpu.make_async_remote_copy(
            src_ref=src,
            dst_ref=dst,
            send_sem=sem.at[0, slot, h],
            recv_sem=sem.at[1, slot, h],
            device_id={"ctx": to},
            device_id_type=MESH,
        )

    def q_copy(d, h):
        return remote(proj.at[h, 1], qb.at[d, h], q_sem, d - 1, h, lax.rem(me + 4 - d, 4))

    def g_copy(d, h):
        return remote(gb.at[0, h], gb.at[d, h], g_sem, d - 1, h, lax.rem(me + 4 - d, 4))

    def y_copy(d, h):
        return remote(yout.at[d - 1, h], yin.at[d - 1, h], y_sem, d - 1, h, lax.rem(me + d, 4))

    def dq_copy(d, h):
        return remote(dqout.at[d - 1, h], dqin.at[d - 1, h], dq_sem, d - 1, h, lax.rem(me + d, 4))

    def kv_copy(h):
        return remote(
            proj.at[h, pl.ds(2, 2)], kb.at[1, h], kv_sem, 0, h, lax.rem(me + 1, 4)
        )

    def dkv_copy(h):
        return remote(
            dkvout.at[h], dkvin.at[h], dkv_sem, 0, h, lax.rem(me + 3, 4)
        )

    for h in range(heads):
        for d in (2, 1):

            @pl.when(asks[d])
            def _():
                q_copy(d, h).start()

        @pl.when(me == 0)
        def _():
            kv_copy(h).start()

    qb[0] = proj[:, 1]
    kb[0] = proj[:, 2:4]

    def run_row(source, index):
        rowbuf[0:1] = source
        return rowbuf[0:1, pl.ds(pl.multiple_of(index * block, block), block)]

    def down(row):
        return jnp.broadcast_to(row, (width, block)).T

    ids = items[...]
    place = lax.broadcasted_iota(jnp.int32, (1, total), 1)
    fresh = (pltpu.roll(ids, total - 1, 1) != ids) & (place < total - 1)
    loss = weights[...]
    loss = loss * jnp.where(fresh, 1.0, 0.0) * total / jnp.sum(loss)
    cmat[...] = down(run_row(loss, me))

    def fill(pair, carry):
        qi, kj = pair // 2, lax.rem(pair, 2)

        @pl.when((qi < n_q) & (kj < n_kv(qi)))
        def _():
            fill_one(pair, me + qi, me - kj)

        return carry

    def fill_one(pair, bq, bk):
        row = run_row(sessions[...].astype(jnp.float32), bq)
        col = down(run_row(sessions[...].astype(jnp.float32), bk))
        col = jnp.concatenate([col] * (block // width), 1)
        full = jnp.float32(0.0)
        for slot in range(lists.shape[0]):
            full = jnp.maximum(full, jnp.where(lists[slot, 0, bq] == bk, 1.0, 0.0))
        c = lax.broadcasted_iota(jnp.int32, (block, block), 0)
        a = lax.broadcasted_iota(jnp.int32, (block, block), 1)
        ahead = a - c + (bq - bk) * block
        window = (ahead >= 0) & (ahead < block)
        near = jnp.where(window & (row == col), 1.0, 0.0)
        mask[pair] = jnp.maximum(near, full).astype(jnp.bfloat16)

    lax.fori_loop(0, 6, fill, 0)

    def forward(h, carry):
        def one_q(qi, carry):
            @pl.when((qi == 1) & (me == 1))
            def _():
                kv_copy(h).wait_recv()

            for d in (1, 2):

                @pl.when((qi == d) & helps[d])
                def _():
                    q_copy(d, h).wait_recv()

            acc[...] = jnp.zeros_like(acc)
            query = qb[qi, h]

            def one_k(kj, carry):
                pair = qi * 2 + kj
                for t in range(chunks):
                    part = pl.ds(t * step, step)
                    raw = dot(kb[kj, h, 0, part], query, NT)
                    sigma = 0.5 * jnp.tanh(raw * (0.5 * scale)) + 0.5
                    prob = raw * scale * sigma
                    slope = sigma + prob * (1.0 - sigma)
                    seen = mask[pair, part]
                    prob = prob.astype(jnp.bfloat16) * seen
                    ptab[pair, h, part] = prob
                    stab[pair, h, part] = slope.astype(jnp.bfloat16) * seen
                acc[...] += dot(kb[kj, h, 1], ptab[pair, h], TN)
                return carry

            lax.fori_loop(0, n_kv(qi), one_k, 0)

            @pl.when(qi == 0)
            def _():
                yown[h] = acc[...].T

            for d in (1, 2):

                @pl.when((qi == d) & helps[d])
                def _():
                    yout[d - 1, h] = acc[...].T.astype(jnp.bfloat16)
                    y_copy(d, h).start()

            return carry

        return lax.fori_loop(0, n_q, one_q, carry)

    lax.fori_loop(0, heads, forward, 0)

    def norm(h, carry):
        for d in (1, 2):

            @pl.when(asks[d])
            def _():
                y_copy(d, h).wait_recv()
                yown[h] = yown[h] + yin[d - 1, h].astype(jnp.float32)

        y = yown[h]
        centre = jnp.mean(y, -1, keepdims=True)
        shifted = y - centre
        inv_std = lax.rsqrt(jnp.mean(shifted * shifted, -1, keepdims=True) + 1e-05)
        normed = shifted * inv_std
        gate = proj[h, 0].astype(jnp.float32)
        mixed[h] = (normed * gate).astype(jnp.bfloat16)
        grad_mixed = cmat[...] * up[h].astype(jnp.float32)
        grads[h, 0] = (grad_mixed * normed).astype(jnp.bfloat16)
        grad_normed = grad_mixed * gate
        grad_att = inv_std * (
            grad_normed
            - jnp.mean(grad_normed, -1, keepdims=True)
            - normed * jnp.mean(grad_normed * normed, -1, keepdims=True)
        )
        gb[0, h] = grad_att.astype(jnp.bfloat16)
        for d in (2, 1):

            @pl.when(asks[d])
            def _():
                g_copy(d, h).start()

        return carry

    lax.fori_loop(0, heads, norm, 0)

    def backward(h, carry):
        dkv[...] = jnp.zeros_like(dkv)

        def one_q(qi, carry):
            for d in (1, 2):

                @pl.when((qi == d) & helps[d])
                def _():
                    g_copy(d, h).wait_recv()

            acc[...] = jnp.zeros_like(acc)
            query = qb[qi, h]
            grad = gb[qi, h]

            def one_k(kj, carry):
                pair = qi * 2 + kj
                for t in range(chunks):
                    part = pl.ds(t * step, step)
                    dprod = dot(kb[kj, h, 1, part], grad, NT)
                    edge = (dprod * stab[pair, h, part].astype(jnp.float32)).astype(jnp.bfloat16)
                    edges[part] = edge
                    dkv[kj, 0, part] += dot(edge, query, NN)
                    dkv[kj, 1, part] += dot(ptab[pair, h, part], grad, NN)
                acc[...] += dot(kb[kj, h, 0], edges[...], TN)
                return carry

            lax.fori_loop(0, n_kv(qi), one_k, 0)

            @pl.when(qi == 0)
            def _():
                yown[h] = acc[...].T * scale

            for d in (1, 2):

                @pl.when((qi == d) & helps[d])
                def _():
                    dqout[d - 1, h] = (acc[...].T * scale).astype(jnp.bfloat16)
                    dq_copy(d, h).start()

            return carry

        lax.fori_loop(0, n_q, one_q, 0)

        @pl.when(me == 1)
        def _():
            dkvout[h, 0] = (dkv[1, 0] * scale).astype(jnp.bfloat16)
            dkvout[h, 1] = dkv[1, 1].astype(jnp.bfloat16)
            dkv_copy(h).start()

        dkvown[h, 0] = dkv[0, 0] * scale
        dkvown[h, 1] = dkv[0, 1]
        return carry

    lax.fori_loop(0, heads, backward, 0)

    def finish(h, carry):
        for d in (1, 2):

            @pl.when(asks[d])
            def _():
                dq_copy(d, h).wait_recv()
                yown[h] = yown[h] + dqin[d - 1, h].astype(jnp.float32)

        @pl.when(me == 0)
        def _():
            dkv_copy(h).wait_recv()
            dkvown[h] = dkvown[h] + dkvin[h].astype(jnp.float32)

        grads[h, 1] = yown[h].astype(jnp.bfloat16)
        grads[h, 2:4] = dkvown[h].astype(jnp.bfloat16)
        return carry

    lax.fori_loop(0, heads, finish, 0)

    def drain(h, carry):
        for d in (1, 2):

            @pl.when(asks[d])
            def _():
                q_copy(d, h).wait_send()
                g_copy(d, h).wait_send()

            @pl.when(helps[d])
            def _():
                y_copy(d, h).wait_send()
                dq_copy(d, h).wait_send()

        @pl.when(me == 0)
        def _():
            kv_copy(h).wait_send()

        @pl.when(me == 1)
        def _():
            dkv_copy(h).wait_send()

        return carry

    lax.fori_loop(0, heads, drain, 0)


def four_shards(projected, upstream, ips_weight, item_ids, session_ids, session_blocks):
    rows = projected[0]
    count, heads, _, width = rows.shape
    proj = jnp.transpose(rows, (1, 2, 0, 3))
    up = jnp.transpose(upstream[0], (1, 0, 2))
    lists = jnp.transpose(session_blocks, (2, 0, 1))
    bf, f32 = jnp.bfloat16, jnp.float32
    vmem = pl.BlockSpec(memory_space=pltpu.VMEM)
    piece = (heads, count, width)
    sems = pltpu.SemaphoreType.DMA
    mixed, grads = pl.pallas_call(
        functools.partial(four_kernel, heads),
        out_shape=(
            jax.ShapeDtypeStruct(piece, bf),
            jax.ShapeDtypeStruct((heads, 4, count, width), bf),
        ),
        in_specs=[vmem] * 5 + [pl.BlockSpec(memory_space=pltpu.SMEM)],
        out_specs=(vmem, vmem),
        scratch_shapes=[
            pltpu.VMEM((3,) + piece, bf),
            pltpu.VMEM((2, heads, 2, count, width), bf),
            pltpu.VMEM((3,) + piece, bf),
            pltpu.VMEM((2,) + piece, bf),
            pltpu.VMEM((2,) + piece, bf),
            pltpu.VMEM((2,) + piece, bf),
            pltpu.VMEM((2,) + piece, bf),
            pltpu.VMEM((heads, 2, count, width), bf),
            pltpu.VMEM((heads, 2, count, width), bf),
            pltpu.VMEM((6, heads, count, count), bf),
            pltpu.VMEM((6, heads, count, count), bf),
            pltpu.VMEM((6, count, count), bf),
            pltpu.VMEM(piece, f32),
            pltpu.VMEM((width, count), f32),
            pltpu.VMEM((2, 2, count, width), f32),
            pltpu.VMEM((heads, 2, count, width), f32),
            pltpu.VMEM((8, ips_weight.shape[1]), f32),
            pltpu.VMEM((count, width), f32),
            pltpu.VMEM((count, count), bf),
            sems((2, 2, heads)),
            sems((2, 2, heads)),
            sems((2, 2, heads)),
            sems((2, 2, heads)),
            sems((2, 1, heads)),
            sems((2, 1, heads)),
        ],
        compiler_params=pltpu.CompilerParams(
            collective_id=0, has_side_effects=True, vmem_limit_bytes=60 * 1024 * 1024
        ),
    )(proj, up, ips_weight, item_ids, session_ids, lists)
    mixed = jnp.transpose(mixed, (1, 0, 2))
    grads = jnp.transpose(grads, (2, 0, 1, 3))
    return (mixed[None], grads[None])


def solution(mesh):
    body = four_shards if mesh.shape["ctx"] == 4 else shards
    placed = (
        P(("groups", "user"), "ctx", "head", None, None),
        P(("groups", "user"), "ctx", "head", None),
        P(("groups", "user"), None),
        P(("groups", "user"), None),
        P(("groups", "user"), None),
        P(("groups", "user"), None, None),
    )
    return jax.shard_map(
        body,
        mesh=mesh,
        in_specs=placed,
        out_specs=(
            P(("groups", "user"), "ctx", "head", None),
            P(("groups", "user"), "ctx", "head", None, None),
        ),
        check_vma=False,
    )
```

```python
import functools
import jax
import jax.numpy as jnp
from jax import lax
from jax.experimental import pallas as pl
from jax.experimental.pallas import tpu as pltpu
from jax.sharding import PartitionSpec as P

BLOCK = 512


def shifted_2(block, axis, distance):
    devices = range(lax.axis_size(axis))
    route = [(i - distance, i) for i in devices if i - distance in devices]
    return lax.ppermute(block, axis, route)


def pair_scores(queries, keys):
    scale = queries.shape[-1] ** (-0.5)
    return jnp.einsum("ahd,chd->hac", queries, keys, preferred_element_type=jnp.float32) * scale


def attend(queries, keys, values, visible):
    scores = pair_scores(queries, keys)
    probs = jnp.where(visible[None], jax.nn.silu(scores), 0.0).astype(jnp.bfloat16)
    return jnp.einsum("hac,chd->ahd", probs, values, preferred_element_type=jnp.float32)


def attend_back(queries, grad_rows, keys, values, visible):
    scale = queries.shape[-1] ** (-0.5)
    scores = pair_scores(queries, keys)
    sigma = jax.nn.sigmoid(scores)
    probs = jnp.where(visible[None], jax.nn.silu(scores), 0.0).astype(jnp.bfloat16)
    slope = sigma * (1.0 + scores * (1.0 - sigma))
    dprod = jnp.einsum("ahd,chd->hac", grad_rows, values, preferred_element_type=jnp.float32)
    edges = jnp.where(visible[None], dprod * slope, 0.0).astype(jnp.bfloat16)
    grad_q = jnp.einsum("hac,chd->ahd", edges, keys, preferred_element_type=jnp.float32) * scale
    grad_k = jnp.einsum("hac,ahd->chd", edges, queries, preferred_element_type=jnp.float32) * scale
    grad_v = jnp.einsum("hac,ahd->chd", probs, grad_rows, preferred_element_type=jnp.float32)
    return (grad_q, grad_k, grad_v)


def shards(projected, upstream, ips_weight, item_ids, session_ids, session_blocks):
    rows = projected[0]
    count = rows.shape[0]
    heads = rows.shape[1]
    width = rows.shape[3]
    block = BLOCK
    local_blocks = count // block
    ctx_rank = lax.axis_index("ctx")
    first = ctx_rank * local_blocks
    sessions = session_ids[0]
    lists = session_blocks[0]
    gates = rows[:, :, 0]
    queries = rows[:, :, 1].reshape(local_blocks, block, heads, width)
    pairs = rows[:, :, 2:4]
    pair_blocks = pairs.reshape(local_blocks, block, heads, 2, width)
    inner = jnp.arange(block)
    below = inner[None, :] <= inner[:, None]
    everything = jnp.ones((block, block), bool)

    def session_slice(index):
        return lax.dynamic_slice_in_dim(sessions, jnp.maximum(index, 0) * block, block)

    list_rows = []
    local = 0
    glob = first + local
    here = session_slice(glob)
    there = session_slice(glob - 1)
    list_row = lax.dynamic_index_in_dim(lists, glob, 0, keepdims=False)
    prev_listed = jnp.any(list_row == glob - 1)
    own_masks = [below & (here[:, None] == here[None, :])]
    prev_masks = [
        jnp.logical_not(below)
        & (here[:, None] == there[None, :])
        & (glob > 0)
        & jnp.logical_not(prev_listed)
    ]
    list_rows.append(list_row)
    previous = shifted_2(pair_blocks[local_blocks - 1], "ctx", 1)
    prior = [previous] + [pair_blocks[local] for local in range(local_blocks - 1)]
    local = 0
    current = pair_blocks[local]
    total = attend(queries[local], current[:, :, 0], current[:, :, 1], own_masks[local])
    total = total + attend(
        queries[local], prior[local][:, :, 0], prior[local][:, :, 1], prev_masks[local]
    )
    totals = [total]
    piece_blocks = lax.all_gather(pairs, "ctx", axis=0, tiled=True).reshape(
        -1, block, heads, 2, width
    )

    def visit(index, acc):
        chosen = lax.dynamic_index_in_dim(piece_blocks, index, 0, keepdims=False)
        local = 0
        hit = jnp.any(list_rows[local] == index)
        updated = [
            lax.cond(
                hit,
                lambda value, local=local: value
                + attend(queries[local], chosen[:, :, 0], chosen[:, :, 1], everything),
                lambda value: value,
                acc[local],
            )
        ]
        return tuple(updated)

    summed = lax.fori_loop(0, piece_blocks.shape[0], visit, tuple(totals))
    attended = summed[0]
    centre = jnp.mean(attended, -1, keepdims=True)
    shifted = attended - centre
    inv_std = lax.rsqrt(jnp.mean(shifted * shifted, -1, keepdims=True) + 1e-05)
    normed = shifted * inv_std
    gates_f = gates.astype(jnp.float32)
    mixed = (normed * gates_f).astype(jnp.bfloat16)
    weights_row = ips_weight[0]
    items = item_ids[0]
    fresh = jnp.concatenate(
        [(items[1:] != items[:-1]).astype(jnp.float32), jnp.zeros((1,), jnp.float32)]
    )
    scaled = weights_row * fresh * weights_row.shape[0] / jnp.sum(weights_row)
    local_scale = lax.dynamic_slice_in_dim(scaled, ctx_rank * count, count)
    grad_mixed = local_scale[:, None, None] * upstream[0].astype(jnp.float32)
    grad_gates = (grad_mixed * normed).astype(jnp.bfloat16)
    grad_normed = grad_mixed * gates_f
    grad_att = inv_std * (
        grad_normed
        - jnp.mean(grad_normed, -1, keepdims=True)
        - normed * jnp.mean(grad_normed * normed, -1, keepdims=True)
    )
    grad_flat = grad_att.astype(jnp.bfloat16)
    grad_rows = grad_flat.reshape(local_blocks, block, heads, width)
    grad_q = []
    grad_kv = []
    local = 0
    current = pair_blocks[local]
    own_q, own_k, own_v = attend_back(
        queries[local], grad_rows[local], current[:, :, 0], current[:, :, 1], own_masks[local]
    )
    near_q, near_k, near_v = attend_back(
        queries[local],
        grad_rows[local],
        prior[local][:, :, 0],
        prior[local][:, :, 1],
        prev_masks[local],
    )
    grad_q.append(own_q + near_q)
    grad_kv.append(jnp.stack([own_k, own_v], 2))
    backward_prev = jnp.stack([near_k, near_v], 2)
    incoming = shifted_2(backward_prev.astype(jnp.bfloat16), "ctx", -1).astype(jnp.float32)
    grad_kv[local_blocks - 1] = grad_kv[local_blocks - 1] + incoming
    pulled = jnp.stack([rows[:, :, 1], grad_flat], 2)
    piece_pairs = lax.all_gather(pairs, "ctx", axis=0, tiled=True).reshape(
        -1, block, heads, 2, width
    )
    piece_pulled = lax.all_gather(pulled, "ctx", axis=0, tiled=True).reshape(
        -1, block, heads, 2, width
    )

    def visit(index, acc):
        sums, owned = acc
        chosen = lax.dynamic_index_in_dim(piece_pairs, index, 0, keepdims=False)
        asked = lax.dynamic_index_in_dim(piece_pulled, index, 0, keepdims=False)
        target_list = lax.dynamic_index_in_dim(lists, index, 0, keepdims=False)
        local = 0
        hit = jnp.any(list_rows[local] == index)
        new_sums = [
            lax.cond(
                hit,
                lambda value, local=local: value
                + attend_back(
                    queries[local], grad_rows[local], chosen[:, :, 0], chosen[:, :, 1], everything
                )[0],
                lambda value: value,
                sums[local],
            )
        ]
        mine = jnp.any(target_list == first + local)

        def owner_add(value, local=local):
            part_q, part_k, part_v = attend_back(
                asked[:, :, 0],
                asked[:, :, 1],
                pair_blocks[local][:, :, 0],
                pair_blocks[local][:, :, 1],
                everything,
            )
            return value + jnp.stack([part_k, part_v], 2)

        new_owned = [lax.cond(mine, owner_add, lambda value: value, owned[local])]
        return (tuple(new_sums), tuple(new_owned))

    sums, owned = lax.fori_loop(0, piece_pairs.shape[0], visit, (tuple(grad_q), tuple(grad_kv)))
    grad_q = list(sums)
    grad_kv = list(owned)
    grad_q_all = grad_q[0].astype(jnp.bfloat16)
    grad_kv_all = grad_kv[0].astype(jnp.bfloat16)
    result = jnp.concatenate([grad_gates[:, :, None], grad_q_all[:, :, None], grad_kv_all], 2)
    return (mixed[None], result[None])


MESH = pl.DeviceIdType.MESH
NT = (((1,), (1,)), ((), ()))
TN = (((0,), (0,)), ((), ()))
NN = (((1,), (0,)), ((), ()))


def dot(a, b, dims):
    return lax.dot_general(a, b, dims, preferred_element_type=jnp.float32)


def four_kernel(
    heads,
    proj,
    up,
    weights,
    items,
    sessions,
    lists,
    mixed,
    grads,
    qb,
    kb,
    gb,
    yin,
    yout,
    dqin,
    dqout,
    dkvin,
    dkvout,
    ptab,
    stab,
    mask,
    yown,
    acc,
    dkv,
    dkvown,
    rowbuf,
    cmat,
    edges,
    q_sem,
    y_sem,
    g_sem,
    dq_sem,
    kv_sem,
    dkv_sem,
):
    me = lax.axis_index("ctx")
    block, width = up.shape[1], up.shape[2]
    total = weights.shape[1]
    scale = width ** (-0.5)
    chunks = 2
    step = block // chunks

    n_q = jnp.where(me == 1, 3, jnp.where(me == 3, 1, 2))

    def n_kv(qi):
        return jnp.where((me == 1) & (qi > 0), 2, 1)

    asks = {1: me >= 1, 2: me == 3}
    helps = {1: me <= 2, 2: me == 1}

    barrier = pltpu.get_barrier_semaphore()
    for d in range(1, 4):
        pl.semaphore_signal(
            barrier, inc=1, device_id={"ctx": lax.rem(me + d, 4)}, device_id_type=MESH
        )
    pl.semaphore_wait(barrier, 3)

    def remote(src, dst, sem, slot, h, to):
        return pltpu.make_async_remote_copy(
            src_ref=src,
            dst_ref=dst,
            send_sem=sem.at[0, slot, h],
            recv_sem=sem.at[1, slot, h],
            device_id={"ctx": to},
            device_id_type=MESH,
        )

    def q_copy(d, h):
        return remote(proj.at[h, 1], qb.at[d, h], q_sem, d - 1, h, lax.rem(me + 4 - d, 4))

    def g_copy(d, h):
        return remote(gb.at[0, h], gb.at[d, h], g_sem, d - 1, h, lax.rem(me + 4 - d, 4))

    def y_copy(d, h):
        return remote(yout.at[d - 1, h], yin.at[d - 1, h], y_sem, d - 1, h, lax.rem(me + d, 4))

    def dq_copy(d, h):
        return remote(dqout.at[d - 1, h], dqin.at[d - 1, h], dq_sem, d - 1, h, lax.rem(me + d, 4))

    def kv_copy(h):
        return remote(
            proj.at[h, pl.ds(2, 2)], kb.at[1, h], kv_sem, 0, h, lax.rem(me + 1, 4)
        )

    def dkv_copy(h):
        return remote(
            dkvout.at[h], dkvin.at[h], dkv_sem, 0, h, lax.rem(me + 3, 4)
        )

    for h in range(heads):
        for d in (2, 1):

            @pl.when(asks[d])
            def _():
                q_copy(d, h).start()

        @pl.when(me == 0)
        def _():
            kv_copy(h).start()

    qb[0] = proj[:, 1]
    kb[0] = proj[:, 2:4]

    def run_row(source, index):
        rowbuf[0:1] = source
        return rowbuf[0:1, pl.ds(pl.multiple_of(index * block, block), block)]

    def down(row):
        return jnp.broadcast_to(row, (width, block)).T

    ids = items[...]
    place = lax.broadcasted_iota(jnp.int32, (1, total), 1)
    fresh = (pltpu.roll(ids, total - 1, 1) != ids) & (place < total - 1)
    loss = weights[...]
    loss = loss * jnp.where(fresh, 1.0, 0.0) * total / jnp.sum(loss)
    cmat[...] = down(run_row(loss, me))

    def fill(pair, carry):
        qi, kj = pair // 2, lax.rem(pair, 2)

        @pl.when((qi < n_q) & (kj < n_kv(qi)))
        def _():
            fill_one(pair, me + qi, me - kj)

        return carry

    def fill_one(pair, bq, bk):
        row = run_row(sessions[...].astype(jnp.float32), bq)
        col = down(run_row(sessions[...].astype(jnp.float32), bk))
        col = jnp.concatenate([col] * (block // width), 1)
        full = jnp.float32(0.0)
        for slot in range(lists.shape[0]):
            full = jnp.maximum(full, jnp.where(lists[slot, 0, bq] == bk, 1.0, 0.0))
        c = lax.broadcasted_iota(jnp.int32, (block, block), 0)
        a = lax.broadcasted_iota(jnp.int32, (block, block), 1)
        ahead = a - c + (bq - bk) * block
        window = (ahead >= 0) & (ahead < block)
        near = jnp.where(window & (row == col), 1.0, 0.0)
        mask[pair] = jnp.maximum(near, full).astype(jnp.bfloat16)

    lax.fori_loop(0, 6, fill, 0)

    def forward(h, carry):
        def one_q(qi, carry):
            @pl.when((qi == 1) & (me == 1))
            def _():
                kv_copy(h).wait_recv()

            for d in (1, 2):

                @pl.when((qi == d) & helps[d])
                def _():
                    q_copy(d, h).wait_recv()

            acc[...] = jnp.zeros_like(acc)
            query = qb[qi, h]

            def one_k(kj, carry):
                pair = qi * 2 + kj
                for t in range(chunks):
                    part = pl.ds(t * step, step)
                    raw = dot(kb[kj, h, 0, part], query, NT)
                    sigma = 0.5 * jnp.tanh(raw * (0.5 * scale)) + 0.5
                    prob = raw * scale * sigma
                    slope = sigma + prob * (1.0 - sigma)
                    seen = mask[pair, part]
                    prob = prob.astype(jnp.bfloat16) * seen
                    ptab[pair, h, part] = prob
                    stab[pair, h, part] = slope.astype(jnp.bfloat16) * seen
                acc[...] += dot(kb[kj, h, 1], ptab[pair, h], TN)
                return carry

            lax.fori_loop(0, n_kv(qi), one_k, 0)

            @pl.when(qi == 0)
            def _():
                yown[h] = acc[...].T

            for d in (1, 2):

                @pl.when((qi == d) & helps[d])
                def _():
                    yout[d - 1, h] = acc[...].T.astype(jnp.bfloat16)
                    y_copy(d, h).start()

            return carry

        return lax.fori_loop(0, n_q, one_q, carry)

    lax.fori_loop(0, heads, forward, 0)

    def norm(h, carry):
        for d in (1, 2):

            @pl.when(asks[d])
            def _():
                y_copy(d, h).wait_recv()
                yown[h] = yown[h] + yin[d - 1, h].astype(jnp.float32)

        y = yown[h]
        centre = jnp.mean(y, -1, keepdims=True)
        shifted = y - centre
        inv_std = lax.rsqrt(jnp.mean(shifted * shifted, -1, keepdims=True) + 1e-05)
        normed = shifted * inv_std
        gate = proj[h, 0].astype(jnp.float32)
        mixed[h] = (normed * gate).astype(jnp.bfloat16)
        grad_mixed = cmat[...] * up[h].astype(jnp.float32)
        grads[h, 0] = (grad_mixed * normed).astype(jnp.bfloat16)
        grad_normed = grad_mixed * gate
        grad_att = inv_std * (
            grad_normed
            - jnp.mean(grad_normed, -1, keepdims=True)
            - normed * jnp.mean(grad_normed * normed, -1, keepdims=True)
        )
        gb[0, h] = grad_att.astype(jnp.bfloat16)
        for d in (2, 1):

            @pl.when(asks[d])
            def _():
                g_copy(d, h).start()

        return carry

    lax.fori_loop(0, heads, norm, 0)

    def backward(h, carry):
        dkv[...] = jnp.zeros_like(dkv)

        def one_q(qi, carry):
            for d in (1, 2):

                @pl.when((qi == d) & helps[d])
                def _():
                    g_copy(d, h).wait_recv()

            acc[...] = jnp.zeros_like(acc)
            query = qb[qi, h]
            grad = gb[qi, h]

            def one_k(turn, carry):
                kj = n_kv(qi) - 1 - turn
                pair = qi * 2 + kj
                for t in range(chunks):
                    part = pl.ds(t * step, step)
                    dprod = dot(kb[kj, h, 1, part], grad, NT)
                    edge = (dprod * stab[pair, h, part].astype(jnp.float32)).astype(jnp.bfloat16)
                    edges[part] = edge
                    dkv[kj, 0, part] += dot(edge, query, NN)
                    dkv[kj, 1, part] += dot(ptab[pair, h, part], grad, NN)

                @pl.when((me == 1) & (qi == 2) & (kj == 1))
                def _():
                    dkvout[h, 0] = (dkv[1, 0] * scale).astype(jnp.bfloat16)
                    dkvout[h, 1] = dkv[1, 1].astype(jnp.bfloat16)
                    dkv_copy(h).start()

                acc[...] += dot(kb[kj, h, 0], edges[...], TN)
                return carry

            lax.fori_loop(0, n_kv(qi), one_k, 0)

            @pl.when(qi == 0)
            def _():
                yown[h] = acc[...].T * scale

            for d in (1, 2):

                @pl.when((qi == d) & helps[d])
                def _():
                    dqout[d - 1, h] = (acc[...].T * scale).astype(jnp.bfloat16)
                    dq_copy(d, h).start()

            return carry

        lax.fori_loop(0, n_q, one_q, 0)

        dkvown[h, 0] = dkv[0, 0] * scale
        dkvown[h, 1] = dkv[0, 1]
        return carry

    lax.fori_loop(0, heads, backward, 0)

    def finish(h, carry):
        for d in (1, 2):

            @pl.when(asks[d])
            def _():
                dq_copy(d, h).wait_recv()
                yown[h] = yown[h] + dqin[d - 1, h].astype(jnp.float32)

        @pl.when(me == 0)
        def _():
            dkv_copy(h).wait_recv()
            dkvown[h] = dkvown[h] + dkvin[h].astype(jnp.float32)

        grads[h, 1] = yown[h].astype(jnp.bfloat16)
        grads[h, 2:4] = dkvown[h].astype(jnp.bfloat16)
        return carry

    lax.fori_loop(0, heads, finish, 0)

    def drain(h, carry):
        for d in (1, 2):

            @pl.when(asks[d])
            def _():
                q_copy(d, h).wait_send()
                g_copy(d, h).wait_send()

            @pl.when(helps[d])
            def _():
                y_copy(d, h).wait_send()
                dq_copy(d, h).wait_send()

        @pl.when(me == 0)
        def _():
            kv_copy(h).wait_send()

        @pl.when(me == 1)
        def _():
            dkv_copy(h).wait_send()

        return carry

    lax.fori_loop(0, heads, drain, 0)


def four_shards(projected, upstream, ips_weight, item_ids, session_ids, session_blocks):
    rows = projected[0]
    count, heads, _, width = rows.shape
    proj = jnp.transpose(rows, (1, 2, 0, 3))
    up = jnp.transpose(upstream[0], (1, 0, 2))
    lists = jnp.transpose(session_blocks, (2, 0, 1))
    bf, f32 = jnp.bfloat16, jnp.float32
    vmem = pl.BlockSpec(memory_space=pltpu.VMEM)
    piece = (heads, count, width)
    sems = pltpu.SemaphoreType.DMA
    mixed, grads = pl.pallas_call(
        functools.partial(four_kernel, heads),
        out_shape=(
            jax.ShapeDtypeStruct(piece, bf),
            jax.ShapeDtypeStruct((heads, 4, count, width), bf),
        ),
        in_specs=[vmem] * 5 + [pl.BlockSpec(memory_space=pltpu.SMEM)],
        out_specs=(vmem, vmem),
        scratch_shapes=[
            pltpu.VMEM((3,) + piece, bf),
            pltpu.VMEM((2, heads, 2, count, width), bf),
            pltpu.VMEM((3,) + piece, bf),
            pltpu.VMEM((2,) + piece, bf),
            pltpu.VMEM((2,) + piece, bf),
            pltpu.VMEM((2,) + piece, bf),
            pltpu.VMEM((2,) + piece, bf),
            pltpu.VMEM((heads, 2, count, width), bf),
            pltpu.VMEM((heads, 2, count, width), bf),
            pltpu.VMEM((6, heads, count, count), bf),
            pltpu.VMEM((6, heads, count, count), bf),
            pltpu.VMEM((6, count, count), bf),
            pltpu.VMEM(piece, f32),
            pltpu.VMEM((width, count), f32),
            pltpu.VMEM((2, 2, count, width), f32),
            pltpu.VMEM((heads, 2, count, width), f32),
            pltpu.VMEM((8, ips_weight.shape[1]), f32),
            pltpu.VMEM((count, width), f32),
            pltpu.VMEM((count, count), bf),
            sems((2, 2, heads)),
            sems((2, 2, heads)),
            sems((2, 2, heads)),
            sems((2, 2, heads)),
            sems((2, 1, heads)),
            sems((2, 1, heads)),
        ],
        compiler_params=pltpu.CompilerParams(
            collective_id=0, has_side_effects=True, vmem_limit_bytes=60 * 1024 * 1024
        ),
    )(proj, up, ips_weight, item_ids, session_ids, lists)
    mixed = jnp.transpose(mixed, (1, 0, 2))
    grads = jnp.transpose(grads, (2, 0, 1, 3))
    return (mixed[None], grads[None])


def solution(mesh):
    body = four_shards if mesh.shape["ctx"] == 4 else shards
    placed = (
        P(("groups", "user"), "ctx", "head", None, None),
        P(("groups", "user"), "ctx", "head", None),
        P(("groups", "user"), None),
        P(("groups", "user"), None),
        P(("groups", "user"), None),
        P(("groups", "user"), None, None),
    )
    return jax.shard_map(
        body,
        mesh=mesh,
        in_specs=placed,
        out_specs=(
            P(("groups", "user"), "ctx", "head", None),
            P(("groups", "user"), "ctx", "head", None, None),
        ),
        check_vma=False,
    )
```
